32 devices in a mesh: pair: 8 (over z, y), red: 4 (over x, core).
Axes of the slice: x: 2, y: 2, z: 4, core: 2. Of those that a mesh axis runs over, the one named last changes fastest.
Arguments:
- amplitudes: bfloat16 [64, 64, 8192], P('pair', None, 'red'), may hold values from -6 to 6
- integrals: bfloat16 [8192, 1024], P('red'), may hold values from -0.1875 to 0.1875
- occ_irrep: int32 [64], replicated, may hold values from 0 to 7
- vir_irrep: int32 [512], replicated, may hold values from 0 to 7, as said below
- cd_orbitals: int32 [2, 8192], P(None, 'red'), may hold values from 0 to 511
- ab_orbitals: int32 [2, 1024], P(None, 'pair'), may hold values from 0 to 511, as said below
Outputs:
- residual: bfloat16 [64, 64, 1024], P(None, 'red', 'pair')
The draws below stay inside these ranges and needn't reach their ends.
Inputs may be any that keep to these rules, and one draw needn't show every extreme that they name: `vir_irrep`: D2h irrep labels; each label is held by exactly 64 virtual orbitals. `occ_irrep`: D2h irrep labels. `cd_orbitals`: indices of virtual orbitals. `ab_orbitals`: indices of virtual orbitals; the slab pairs m with m // 128 equal come as 8 blocks of 16 pairs, and ab_irrep[m] = (m % 128) // 16.
All inputs are finite; a program needn't handle non-finite values.
Results may differ from the reference program's by a relative error of at most 0.001.
Values may be sent and summed in bfloat16 or wider, within the bound.
No kernel may reach another device: no remote copies, remote signals or barrier semaphores. Data moves between devices by JAX's collectives and lax.ppermute only.
A program may use at most 192 MiB of HBM per device.

```python
import jax
import jax.numpy as jnp

O = 64
NV = 512
AB_DEV = 128
CD = 8192
AB = 1024


def label_order(key):
    return jax.random.permutation(jax.random.fold_in(key, 11), NV).astype(jnp.int32)


def draw_vir_irrep(key, part):
    return (label_order(key) % 8).astype(jnp.int32)


def draw_ab_orbitals(key, part):
    order = label_order(key)
    inverse = jnp.argsort(order, stable=True).astype(jnp.int32)
    labels = order % 8
    first = jax.random.randint(jax.random.fold_in(key, 12), (AB,), 0, NV).astype(jnp.int32)
    target = jnp.arange(AB, dtype=jnp.int32) % AB_DEV // (AB_DEV // 8)
    wanted = jnp.bitwise_xor(target, labels[first])
    within = jax.random.randint(jax.random.fold_in(key, 13), (AB,), 0, NV // 8).astype(jnp.int32)
    second = inverse[8 * within + wanted]
    return jnp.stack([first, second]).astype(jnp.int32)


def plant(drawn, key, least, top_value):
    shape = drawn.shape
    place = [jax.random.randint(jax.random.fold_in(key, axis), (), 0, shape[axis]) for axis in range(len(shape))]
    drawn = drawn.at[tuple(place)].set(least)
    longest = shape.index(max(shape))
    place[longest] = (place[longest] + 1) % shape[longest]
    return drawn.at[tuple(place)].set(top_value)


def level_of(own_key, extent, shards, least, high):
    level, own = 1.0, jax.random.fold_in(own_key, 6)
    for position, blocks in shards:
        draws = jnp.exp(jax.random.uniform(jax.random.fold_in(own, position), (blocks,), jnp.float32, least / len(shards), high / len(shards)))
        level = level * jnp.repeat(draws, extent[position] // blocks).reshape([-1 if axis == position else 1 for axis in range(len(extent))])
    return level


def gaussian(key, shape, width, bound, cuts=(), held_as=jnp.bfloat16):
    factor_of = level_of(key, shape, cuts, -0.22, 0.18) if cuts else 1.0
    entries = jax.random.normal(key, shape, jnp.float32) * width * factor_of
    return jnp.minimum(jnp.maximum(entries, -bound), bound).astype(held_as)


def setup_inputs(seed: int = 0) -> dict:
    seeds = jax.random.split(jax.random.key(seed), 7)
    amplitudes = gaussian(seeds[0], (O, O, CD), 1.0, 6.0, ((0, 8), (2, 4)))
    integrals = gaussian(seeds[1], (CD, AB), (CD // 8) ** -0.5, 0.1875, ((0, 4),))
    occ_irrep = plant(jax.random.randint(seeds[2], (O,), 0, 8), jax.random.fold_in(seeds[2], 1), 0, 7).astype(jnp.int32)
    vir_irrep = draw_vir_irrep(jax.random.fold_in(seeds[6], 71), 0)
    cd_orbitals = plant(jax.random.randint(seeds[4], (2, CD), 0, NV), jax.random.fold_in(seeds[4], 1), 0, NV - 1).astype(jnp.int32)
    ab_orbitals = draw_ab_orbitals(jax.random.fold_in(seeds[6], 71), 0)
    return {"amplitudes": amplitudes, "integrals": integrals, "occ_irrep": occ_irrep, "vir_irrep": vir_irrep, "cd_orbitals": cd_orbitals, "ab_orbitals": ab_orbitals}


def pair_labels(orbitals, vir_irrep):
    return jnp.bitwise_xor(vir_irrep[orbitals[0]], vir_irrep[orbitals[1]]).astype(jnp.int32)


def reference(amplitudes, integrals, occ_irrep, vir_irrep, cd_orbitals, ab_orbitals):
    pair_irrep = jnp.bitwise_xor(occ_irrep[:, None], occ_irrep[None, :]).astype(jnp.int32)
    cd_irrep = pair_labels(cd_orbitals, vir_irrep)
    ab_irrep = pair_labels(ab_orbitals, vir_irrep)
    masked = jnp.where(pair_irrep[:, :, None] == cd_irrep[None, None, :], amplitudes, jnp.zeros((), amplitudes.dtype))
    ladder = jnp.dot(masked.reshape(O * O, CD), integrals, preferred_element_type=jnp.float32).reshape(O, O, AB)
    kept = jnp.where(pair_irrep[:, :, None] == ab_irrep[None, None, :], ladder, jnp.zeros((), ladder.dtype))
    return kept.astype(jnp.bfloat16)
```

```python
import functools

import jax
import jax.numpy as jnp
from jax import lax
from jax.experimental import pallas as pl
from jax.experimental.pallas import tpu as pltpu
from jax.sharding import PartitionSpec as P

LABELS = 8
LANES = 128
BLOCK = LANES // LABELS
F32, BF16, I32 = jnp.float32, jnp.bfloat16, jnp.int32


def pair_labels(orbitals, vir_irrep):
    labels = lax.broadcasted_iota(I32, (1, vir_irrep.shape[0]), 1)
    first = jnp.sum(jnp.where(orbitals[0][:, None] == labels, vir_irrep[None, :], 0), axis=1)
    second = jnp.sum(jnp.where(orbitals[1][:, None] == labels, vir_irrep[None, :], 0), axis=1)
    return jnp.bitwise_xor(first, second)


def general(amplitudes, integrals, occ_irrep, vir_irrep, cd_orbitals, ab_orbitals):
    own_rows, occupied, depth = amplitudes.shape
    width = ab_orbitals.shape[1]
    owners = integrals.shape[1] // width
    block = width // LABELS
    own_irrep = lax.dynamic_slice_in_dim(occ_irrep, lax.axis_index("pair") * own_rows, own_rows, 0)
    pair_irrep = jnp.bitwise_xor(own_irrep[:, None], occ_irrep[None, :])
    cd_irrep = pair_labels(cd_orbitals, vir_irrep)
    masked = jnp.where(pair_irrep[:, :, None] == cd_irrep, amplitudes, jnp.zeros((), BF16))
    sums = jnp.dot(
        masked.reshape(own_rows * occupied, depth), integrals, preferred_element_type=F32
    ).reshape(own_rows, occupied, owners, LABELS, block)
    label = lax.broadcasted_iota(I32, (LABELS, 1), 0)
    kept = jnp.where(pair_irrep[:, :, None, None, None] == label, sums, 0.0).sum(axis=3)
    summed = lax.psum_scatter(kept, "red", scatter_dimension=1, tiled=True)
    moved = lax.all_to_all(
        summed.astype(BF16), "pair", split_axis=2, concat_axis=0, tiled=True
    )[:, :, 0, None, :]
    j_rows = moved.shape[1]
    j_irrep = lax.dynamic_slice_in_dim(occ_irrep, lax.axis_index("red") * j_rows, j_rows, 0)
    out_irrep = jnp.bitwise_xor(occ_irrep[:, None], j_irrep[None, :])
    out = jnp.where(out_irrep[:, :, None, None] == label, moved, jnp.zeros((), BF16))
    return out.reshape(occupied, j_rows, width)


OWNERS = 8
REDS = 4
V_CHUNKS = 2


def place(offset):
    bit = [(offset >> b) & 1 for b in range(5)]
    odd = bit[0] ^ bit[1] ^ bit[2] ^ bit[3] ^ bit[4]
    return (((odd * 2 + bit[1]) * 2 + bit[2]) * 2 + bit[3]) * 2 + bit[4]


def pick(vectors, shift_bits):
    for b in range(3):
        vectors = [
            jnp.where(shift_bits[b], vectors[(d + 2**b) % 8], vectors[d]) for d in range(8)
        ]
    return vectors


def turn(vector, blocks):
    return pltpu.roll(vector, blocks % LABELS * BLOCK, 1) if blocks % LABELS else vector


def bits_of(labels):
    return [((labels >> b) & 1) == 1 for b in range(3)]


def sums_kernel(
    occ_hbm, vir_hbm, cd_hbm, t_hbm, v_hbm, keep, give, j_out, i_out,
    t_buf, v_buf, w_buf, total, occ, vir, cd, t_sem, v_sem, s_sem,
):
    rows, occupied, depth = t_buf.shape
    span = depth // V_CHUNKS
    small = [
        pltpu.make_async_copy(source, target, s_sem.at[n])
        for n, (source, target) in enumerate(((occ_hbm, occ), (vir_hbm, vir), (cd_hbm, cd)))
    ]
    v_copies = [
        pltpu.make_async_copy(
            v_hbm.at[pl.ds(c * span, span), :], v_buf.at[pl.ds(c * span, span), :], v_sem.at[c]
        )
        for c in range(V_CHUNKS)
    ]
    t_copy = pltpu.make_async_copy(t_hbm, t_buf, t_sem)
    for copy in (*small, *v_copies, t_copy):
        copy.start()
    pair, red = lax.axis_index("pair"), lax.axis_index("red")
    for copy in small:
        copy.wait()

    zero, one = jnp.zeros((), BF16), jnp.ones((), BF16)
    sublane = lax.broadcasted_iota(I32, (8, LANES), 0)
    lane_block = lax.broadcasted_iota(I32, (8, LANES), 1) // BLOCK

    def column(first):
        value = jnp.full((8, LANES), occ[first], I32)
        for s in range(1, 8):
            value = jnp.where(sublane == s, occ[first + s], value)
        return value

    occ_j = [column(8 * g) for g in range(occupied // 8)]
    occ_j16 = jnp.concatenate(occ_j, 0).astype(F32).astype(BF16)
    occ_i = [occ[pair * rows + i] for i in range(rows)]

    pieces = vir.shape[0] // LANES
    table = [
        jnp.broadcast_to(vir[pl.ds(LANES * n, LANES)].reshape(1, LANES), (8, LANES))
        for n in range(pieces)
    ]
    block_row = (lax.broadcasted_iota(I32, (LANES, LANES), 0) // BLOCK).astype(F32).astype(BF16)
    labels, masks = [], []
    for q in range(depth // LANES):
        index = cd[:, pl.ds(q * LANES, LANES)]
        index = jnp.concatenate([index, jnp.zeros((6, LANES), I32)], 0)
        within, piece = index % LANES, index // LANES
        found = jnp.take_along_axis(table[0], within, axis=1)
        for n in range(1, pieces):
            found = jnp.where(piece == n, jnp.take_along_axis(table[n], within, axis=1), found)
        label = found[0:1] ^ found[1:2]
        labels.append(label)
        spread = jnp.broadcast_to(label, (LANES, LANES)).astype(F32).astype(BF16)
        masks.append(jnp.where(spread == block_row, one, zero).T)

    for c in range(V_CHUNKS):
        v_copies[c].wait()
        for q in range(c * span // LANES, (c + 1) * span // LANES):
            ks = pl.ds(q * LANES, LANES)
            mask = masks[q] != zero
            folded = jnp.where(mask, v_buf[ks, 0:LANES], zero)
            for p in range(1, OWNERS):
                part = jnp.where(mask, v_buf[ks, pl.ds(p * LANES, LANES)], zero)
                folded = folded + turn(part, p)
            w_buf[ks, :] = folded

    t_copy.wait()
    masked = []
    for i in range(rows):
        row = []
        for q in range(depth // LANES):
            wanted = jnp.broadcast_to(labels[q] ^ occ_i[i], (occupied, LANES))
            wanted = wanted.astype(F32).astype(BF16)
            row.append(jnp.where(wanted == occ_j16, t_buf[i, :, pl.ds(q * LANES, LANES)], zero))
        masked.append(jnp.concatenate(row, 1))
    total[...] = jnp.dot(
        jnp.concatenate(masked, 0), w_buf[...], preferred_element_type=F32
    )

    lane_bits = bits_of(lane_block)
    occ_i_lane = jnp.zeros((8, LANES), I32)
    for i in range(rows):
        occ_i_lane = jnp.where(lane_block == i, occ_i[i], occ_i_lane)
    me = pair * REDS + red
    j_rows = occupied // REDS
    for g in range(occupied // 8):
        held = [turn(total[pl.ds(i * occupied + g * 8, 8), :], i) for i in range(rows)]
        skewed = pick(held, lane_bits)
        held = [turn(skewed[-d % 8], -d) for d in range(8)]
        held = pick(held, bits_of(occ_j[g] ^ occ_i_lane))
        for p in range(OWNERS):
            to = place((p * REDS + g * 8 // j_rows) ^ me)
            at = (to % 16, pl.ds(g * 8 % j_rows, 8), slice(None))

            @pl.when(to < 16)
            def _(p=p, at=at, held=held):
                keep[at] = held[p]

            @pl.when(to >= 16)
            def _(p=p, at=at, held=held):
                give[at] = held[p]

    for g in range(j_rows // 8):
        value = column(red * j_rows + 8 * g) ^ lane_block
        j_out[pl.ds(8 * g, 8), :] = value.astype(F32)
    for a in range(OWNERS):
        i_out[pl.ds(8 * a, 8), :] = column((pair ^ a) * rows).astype(F32)


def spread_kernel(held, came, j_in, i_in, out, buf, sem):
    pair = lax.axis_index("pair")
    lane_block = lax.broadcasted_iota(I32, (1, LANES), 1) // BLOCK
    bits = bits_of(jnp.broadcast_to(lane_block, held.shape[1:]))
    j_side = j_in[...].astype(BF16)
    copies = []
    for a in range(OWNERS):
        block = (held if a < 4 else came)[a % 4]
        level = [block]
        for b in (2, 1, 0):
            level = [
                jnp.where(bits[b], *((v, turn(v, -(2**b))) if upper else (turn(v, 2**b), v)))
                for v in level
                for upper in (False, True)
            ]
        for i in range(8):
            wanted = jnp.broadcast_to(i_in[pl.ds(8 * a + i, 1), :], j_side.shape).astype(BF16)
            buf[a, i] = jnp.where(wanted == j_side, level[i], jnp.zeros((), BF16))
        copy = pltpu.make_async_copy(buf.at[a], out.at[pl.ds((pair ^ a) * 8, 8)], sem.at[a])
        copy.start()
        copies.append(copy)
    for copy in copies:
        copy.wait()


def in_hbm(*arrays):
    return [pltpu.with_memory_space_constraint(a, pltpu.HBM) for a in arrays]


def fast(amplitudes, integrals, occ_irrep, vir_irrep, cd_orbitals, ab_orbitals):
    rows, occupied, depth = amplitudes.shape
    j_rows = occupied // REDS
    vmem, hbm = pl.BlockSpec(memory_space=pltpu.VMEM), pl.BlockSpec(memory_space=pltpu.HBM)
    half = jax.ShapeDtypeStruct((16, j_rows, LANES), F32)
    keep, give, j_side, i_side = pl.pallas_call(
        sums_kernel,
        out_shape=(
            half,
            half,
            jax.ShapeDtypeStruct((j_rows, LANES), F32),
            jax.ShapeDtypeStruct((occupied, LANES), F32),
        ),
        in_specs=[hbm] * 5,
        out_specs=(vmem,) * 4,
        scratch_shapes=[
            pltpu.VMEM(amplitudes.shape, BF16),
            pltpu.VMEM(integrals.shape, BF16),
            pltpu.VMEM((depth, LANES), BF16),
            pltpu.VMEM((rows * occupied, LANES), F32),
            pltpu.SMEM(occ_irrep.shape, I32),
            pltpu.VMEM(vir_irrep.shape, I32),
            pltpu.VMEM(cd_orbitals.shape, I32),
            pltpu.SemaphoreType.DMA,
            pltpu.SemaphoreType.DMA((V_CHUNKS,)),
            pltpu.SemaphoreType.DMA((3,)),
        ],
        compiler_params=pltpu.CompilerParams(vmem_limit_bytes=32 * 2**20),
        name="sums",
    )(*in_hbm(occ_irrep, vir_irrep, cd_orbitals, amplitudes, integrals))

    def swap(block, pattern):
        pairs = [(d, d ^ pattern) for d in range(OWNERS * REDS)]
        return lax.ppermute(block, ("pair", "red"), pairs)

    chip = keep + swap(give, 0b00001)
    done = (chip[:8] + swap(chip[8:], 0b00011)).astype(BF16)
    came = swap(done[4:], 0b00101)
    both = jnp.stack([done[:4], came]).reshape(2, 2, 2, j_rows, LANES)
    came = swap(both[:, 1], 0b01001)
    both = jnp.stack([both[:, 0], came]).reshape(4, 2, j_rows, LANES)
    held = both[:, 0]
    came = swap(both[:, 1], 0b10001)

    return pl.pallas_call(
        spread_kernel,
        out_shape=jax.ShapeDtypeStruct((occupied, j_rows, LANES), BF16),
        in_specs=[vmem] * 4,
        out_specs=hbm,
        scratch_shapes=[
            pltpu.VMEM((OWNERS, 8, j_rows, LANES), BF16),
            pltpu.SemaphoreType.DMA((OWNERS,)),
        ],
        name="spread",
    )(held, came, j_side, i_side)


def solution(mesh):
    def local(amplitudes, integrals, occ_irrep, vir_irrep, cd_orbitals, ab_orbitals):
        sizes = mesh.shape["pair"], mesh.shape["red"], amplitudes.shape[0], ab_orbitals.shape[1]
        form = fast if sizes == (OWNERS, REDS, 8, LANES) else general
        return form(amplitudes, integrals, occ_irrep, vir_irrep, cd_orbitals, ab_orbitals)

    in_specs = (P("pair", None, "red"), P("red", None), P(), P(), P(None, "red"), P(None, "pair"))
    out_specs = P(None, "red", "pair")
    return jax.shard_map(local, mesh=mesh, in_specs=in_specs, out_specs=out_specs, check_vma=False)
```

```python
import functools

import jax
import jax.numpy as jnp
from jax import lax
from jax.experimental import pallas as pl
from jax.experimental.pallas import tpu as pltpu
from jax.sharding import PartitionSpec as P

LABELS = 8
LANES = 128
BLOCK = LANES // LABELS
F32, BF16, I32 = jnp.float32, jnp.bfloat16, jnp.int32


def pair_labels(orbitals, vir_irrep):
    labels = lax.broadcasted_iota(I32, (1, vir_irrep.shape[0]), 1)
    first = jnp.sum(jnp.where(orbitals[0][:, None] == labels, vir_irrep[None, :], 0), axis=1)
    second = jnp.sum(jnp.where(orbitals[1][:, None] == labels, vir_irrep[None, :], 0), axis=1)
    return jnp.bitwise_xor(first, second)


def general(amplitudes, integrals, occ_irrep, vir_irrep, cd_orbitals, ab_orbitals):
    own_rows, occupied, depth = amplitudes.shape
    width = ab_orbitals.shape[1]
    owners = integrals.shape[1] // width
    block = width // LABELS
    own_irrep = lax.dynamic_slice_in_dim(occ_irrep, lax.axis_index("pair") * own_rows, own_rows, 0)
    pair_irrep = jnp.bitwise_xor(own_irrep[:, None], occ_irrep[None, :])
    cd_irrep = pair_labels(cd_orbitals, vir_irrep)
    masked = jnp.where(pair_irrep[:, :, None] == cd_irrep, amplitudes, jnp.zeros((), BF16))
    sums = jnp.dot(
        masked.reshape(own_rows * occupied, depth), integrals, preferred_element_type=F32
    ).reshape(own_rows, occupied, owners, LABELS, block)
    label = lax.broadcasted_iota(I32, (LABELS, 1), 0)
    kept = jnp.where(pair_irrep[:, :, None, None, None] == label, sums, 0.0).sum(axis=3)
    summed = lax.psum_scatter(kept, "red", scatter_dimension=1, tiled=True)
    moved = lax.all_to_all(
        summed.astype(BF16), "pair", split_axis=2, concat_axis=0, tiled=True
    )[:, :, 0, None, :]
    j_rows = moved.shape[1]
    j_irrep = lax.dynamic_slice_in_dim(occ_irrep, lax.axis_index("red") * j_rows, j_rows, 0)
    out_irrep = jnp.bitwise_xor(occ_irrep[:, None], j_irrep[None, :])
    out = jnp.where(out_irrep[:, :, None, None] == label, moved, jnp.zeros((), BF16))
    return out.reshape(occupied, j_rows, width)


OWNERS = 8
REDS = 4
V_CHUNKS = 2


def place(offset):
    bit = [(offset >> b) & 1 for b in range(5)]
    odd = bit[0] ^ bit[1] ^ bit[2] ^ bit[3] ^ bit[4]
    return (((odd * 2 + bit[1]) * 2 + bit[2]) * 2 + bit[3]) * 2 + bit[4]


def pick(vectors, shift_bits):
    for b in range(3):
        vectors = [
            jnp.where(shift_bits[b], vectors[(d + 2**b) % 8], vectors[d]) for d in range(8)
        ]
    return vectors


def turn(vector, blocks):
    return pltpu.roll(vector, blocks % LABELS * BLOCK, 1) if blocks % LABELS else vector


def bits_of(labels):
    return [((labels >> b) & 1) == 1 for b in range(3)]


def sums_kernel(
    occ_hbm, vir_hbm, cd_hbm, t_hbm, v_hbm, sums, j_out, i_out,
    t_buf, v_buf, w_buf, total, occ, vir, cd, t_sem, v_sem, s_sem,
):
    rows, occupied, depth = t_buf.shape
    span = depth // V_CHUNKS
    small = [
        pltpu.make_async_copy(source, target, s_sem.at[n])
        for n, (source, target) in enumerate(((occ_hbm, occ), (vir_hbm, vir), (cd_hbm, cd)))
    ]
    v_copies = [
        pltpu.make_async_copy(
            v_hbm.at[pl.ds(c * span, span), :], v_buf.at[pl.ds(c * span, span), :], v_sem.at[c]
        )
        for c in range(V_CHUNKS)
    ]
    t_copy = pltpu.make_async_copy(t_hbm, t_buf, t_sem)
    for copy in (*small, *v_copies, t_copy):
        copy.start()
    pair, red = lax.axis_index("pair"), lax.axis_index("red")
    for copy in small:
        copy.wait()

    zero, one = jnp.zeros((), BF16), jnp.ones((), BF16)
    sublane = lax.broadcasted_iota(I32, (8, LANES), 0)
    lane_block = lax.broadcasted_iota(I32, (8, LANES), 1) // BLOCK

    def column(first):
        value = jnp.full((8, LANES), occ[first], I32)
        for s in range(1, 8):
            value = jnp.where(sublane == s, occ[first + s], value)
        return value

    occ_j = [column(8 * g) for g in range(occupied // 8)]
    occ_j16 = jnp.concatenate(occ_j, 0).astype(F32).astype(BF16)
    occ_i = [occ[pair * rows + i] for i in range(rows)]

    j_rows = occupied // REDS
    for g in range(j_rows // 8):
        value = column(red * j_rows + 8 * g) ^ lane_block
        j_out[pl.ds(8 * g, 8), :] = value.astype(F32)
    for a in range(OWNERS):
        i_out[pl.ds(8 * a, 8), :] = column((pair ^ a) * rows).astype(F32)

    pieces = vir.shape[0] // LANES
    table = [
        jnp.broadcast_to(vir[pl.ds(LANES * n, LANES)].reshape(1, LANES), (8, LANES))
        for n in range(pieces)
    ]
    block_row = (lax.broadcasted_iota(I32, (LANES, LANES), 0) // BLOCK).astype(F32).astype(BF16)
    labels, masks = [], []
    for q in range(depth // LANES):
        index = cd[:, pl.ds(q * LANES, LANES)]
        index = jnp.concatenate([index, jnp.zeros((6, LANES), I32)], 0)
        within, piece = index % LANES, index // LANES
        found = jnp.take_along_axis(table[0], within, axis=1)
        for n in range(1, pieces):
            found = jnp.where(piece == n, jnp.take_along_axis(table[n], within, axis=1), found)
        label = found[0:1] ^ found[1:2]
        labels.append(label)
        spread = jnp.broadcast_to(label, (LANES, LANES)).astype(F32).astype(BF16)
        masks.append(jnp.where(spread == block_row, one, zero).T)

    for c in range(V_CHUNKS):
        v_copies[c].wait()
        for q in range(c * span // LANES, (c + 1) * span // LANES):
            ks = pl.ds(q * LANES, LANES)
            mask = masks[q] != zero
            folded = jnp.where(mask, v_buf[ks, 0:LANES], zero)
            for p in range(1, OWNERS):
                part = jnp.where(mask, v_buf[ks, pl.ds(p * LANES, LANES)], zero)
                folded = folded + turn(part, p)
            w_buf[ks, :] = folded

    t_copy.wait()
    masked = []
    for i in range(rows):
        row = []
        for q in range(depth // LANES):
            wanted = jnp.broadcast_to(labels[q] ^ occ_i[i], (occupied, LANES))
            wanted = wanted.astype(F32).astype(BF16)
            row.append(jnp.where(wanted == occ_j16, t_buf[i, :, pl.ds(q * LANES, LANES)], zero))
        masked.append(jnp.concatenate(row, 1))
    total[...] = jnp.dot(
        jnp.concatenate(masked, 0), w_buf[...], preferred_element_type=F32
    )

    lane_bits = bits_of(lane_block)
    occ_i_lane = jnp.zeros((8, LANES), I32)
    for i in range(rows):
        occ_i_lane = jnp.where(lane_block == i, occ_i[i], occ_i_lane)
    me = pair * REDS + red
    for g in range(occupied // 8):
        held = [turn(total[pl.ds(i * occupied + g * 8, 8), :], i) for i in range(rows)]
        skewed = pick(held, lane_bits)
        held = [turn(skewed[-d % 8], -d) for d in range(8)]
        held = pick(held, bits_of(occ_j[g] ^ occ_i_lane))
        for p in range(OWNERS):
            to = place((p * REDS + g * 8 // j_rows) ^ me)
            sums[to, pl.ds(g * 8 % j_rows, 8), :] = held[p]


def spread_kernel(first, blocks, j_in, i_in, *refs):
    out, buf, sem = refs[-3:]
    pair = lax.axis_index("pair")
    lane_block = lax.broadcasted_iota(I32, blocks.shape[1:], 1) // BLOCK
    bits = bits_of(lane_block)
    j_side = j_in[...].astype(BF16)
    copies = []
    for n in range(4):
        a = first + n
        level = [blocks[n]]
        for b in (2, 1, 0):
            level = [
                jnp.where(bits[b], *((v, turn(v, -(2**b))) if upper else (turn(v, 2**b), v)))
                for v in level
                for upper in (False, True)
            ]
        for i in range(8):
            wanted = jnp.broadcast_to(i_in[pl.ds(8 * a + i, 1), :], j_side.shape).astype(BF16)
            buf[n, i] = jnp.where(wanted == j_side, level[i], jnp.zeros((), BF16))
        copy = pltpu.make_async_copy(buf.at[n], out.at[pl.ds((pair ^ a) * 8, 8)], sem.at[n])
        copy.start()
        copies.append(copy)
    for copy in copies:
        copy.wait()


def spread(first, blocks, j_side, i_side, *so_far):
    occupied, j_rows = i_side.shape[0], j_side.shape[0]
    vmem, hbm = pl.BlockSpec(memory_space=pltpu.VMEM), pl.BlockSpec(memory_space=pltpu.HBM)
    return pl.pallas_call(
        functools.partial(spread_kernel, first),
        out_shape=jax.ShapeDtypeStruct((occupied, j_rows, LANES), BF16),
        in_specs=[vmem] * 3 + [hbm] * len(so_far),
        out_specs=hbm,
        scratch_shapes=[
            pltpu.VMEM((4, 8, j_rows, LANES), BF16),
            pltpu.SemaphoreType.DMA((4,)),
        ],
        input_output_aliases={3: 0} if so_far else {},
        compiler_params=pltpu.CompilerParams(vmem_limit_bytes=8 * 2**20),
        cost_estimate=pl.CostEstimate(
            flops=2 * 10**6, bytes_accessed=2 * occupied * j_rows * LANES, transcendentals=0
        ),
        name="spread",
    )(blocks, j_side, i_side, *so_far)


def in_hbm(*arrays):
    return [pltpu.with_memory_space_constraint(a, pltpu.HBM) for a in arrays]


def fast(amplitudes, integrals, occ_irrep, vir_irrep, cd_orbitals, ab_orbitals):
    rows, occupied, depth = amplitudes.shape
    j_rows = occupied // REDS
    vmem, hbm = pl.BlockSpec(memory_space=pltpu.VMEM), pl.BlockSpec(memory_space=pltpu.HBM)
    sums, j_side, i_side = pl.pallas_call(
        sums_kernel,
        out_shape=(
            jax.ShapeDtypeStruct((OWNERS * REDS, j_rows, LANES), F32),
            jax.ShapeDtypeStruct((j_rows, LANES), F32),
            jax.ShapeDtypeStruct((occupied, LANES), F32),
        ),
        in_specs=[hbm] * 5,
        out_specs=(vmem,) * 3,
        scratch_shapes=[
            pltpu.VMEM(amplitudes.shape, BF16),
            pltpu.VMEM(integrals.shape, BF16),
            pltpu.VMEM((depth, LANES), BF16),
            pltpu.VMEM((rows * occupied, LANES), F32),
            pltpu.SMEM(occ_irrep.shape, I32),
            pltpu.VMEM(vir_irrep.shape, I32),
            pltpu.VMEM(cd_orbitals.shape, I32),
            pltpu.SemaphoreType.DMA,
            pltpu.SemaphoreType.DMA((V_CHUNKS,)),
            pltpu.SemaphoreType.DMA((3,)),
        ],
        compiler_params=pltpu.CompilerParams(vmem_limit_bytes=32 * 2**20),
        name="sums",
    )(*in_hbm(occ_irrep, vir_irrep, cd_orbitals, amplitudes, integrals))

    def swap(block, pattern):
        pairs = [(d, d ^ pattern) for d in range(OWNERS * REDS)]
        return lax.ppermute(block, ("pair", "red"), pairs)

    chip = sums[:16] + swap(sums[16:], 0b00001)
    done = (chip[:8] + swap(chip[8:], 0b00011)).astype(BF16)
    came = swap(done[4:], 0b00101)
    both = jnp.stack([done[:4], came]).reshape(2, 2, 2, j_rows, LANES)
    came = swap(both[:, 1], 0b01001)
    both = jnp.stack([both[:, 0], came]).reshape(4, 2, j_rows, LANES)
    held = both[:, 0]
    came = swap(both[:, 1], 0b10001)

    half = spread(0, held, j_side, i_side)
    return spread(4, came, j_side, i_side, half)


def solution(mesh):
    def local(amplitudes, integrals, occ_irrep, vir_irrep, cd_orbitals, ab_orbitals):
        sizes = mesh.shape["pair"], mesh.shape["red"], amplitudes.shape[0], ab_orbitals.shape[1]
        form = fast if sizes == (OWNERS, REDS, 8, LANES) else general
        return form(amplitudes, integrals, occ_irrep, vir_irrep, cd_orbitals, ab_orbitals)

    in_specs = (P("pair", None, "red"), P("red", None), P(), P(), P(None, "red"), P(None, "pair"))
    out_specs = P(None, "red", "pair")
    return jax.shard_map(local, mesh=mesh, in_specs=in_specs, out_specs=out_specs, check_vma=False)
```

```python
import functools

import jax
import jax.numpy as jnp
from jax import lax
from jax.experimental import pallas as pl
from jax.experimental.pallas import tpu as pltpu
from jax.sharding import PartitionSpec as P

LABELS = 8
LANES = 128
BLOCK = LANES // LABELS
F32, BF16, I32 = jnp.float32, jnp.bfloat16, jnp.int32


def pair_labels(orbitals, vir_irrep):
    labels = lax.broadcasted_iota(I32, (1, vir_irrep.shape[0]), 1)
    first = jnp.sum(jnp.where(orbitals[0][:, None] == labels, vir_irrep[None, :], 0), axis=1)
    second = jnp.sum(jnp.where(orbitals[1][:, None] == labels, vir_irrep[None, :], 0), axis=1)
    return jnp.bitwise_xor(first, second)


def general(amplitudes, integrals, occ_irrep, vir_irrep, cd_orbitals, ab_orbitals):
    own_rows, occupied, depth = amplitudes.shape
    width = ab_orbitals.shape[1]
    owners = integrals.shape[1] // width
    block = width // LABELS
    own_irrep = lax.dynamic_slice_in_dim(occ_irrep, lax.axis_index("pair") * own_rows, own_rows, 0)
    pair_irrep = jnp.bitwise_xor(own_irrep[:, None], occ_irrep[None, :])
    cd_irrep = pair_labels(cd_orbitals, vir_irrep)
    masked = jnp.where(pair_irrep[:, :, None] == cd_irrep, amplitudes, jnp.zeros((), BF16))
    sums = jnp.dot(
        masked.reshape(own_rows * occupied, depth), integrals, preferred_element_type=F32
    ).reshape(own_rows, occupied, owners, LABELS, block)
    label = lax.broadcasted_iota(I32, (LABELS, 1), 0)
    kept = jnp.where(pair_irrep[:, :, None, None, None] == label, sums, 0.0).sum(axis=3)
    summed = lax.psum_scatter(kept, "red", scatter_dimension=1, tiled=True)
    moved = lax.all_to_all(
        summed.astype(BF16), "pair", split_axis=2, concat_axis=0, tiled=True
    )[:, :, 0, None, :]
    j_rows = moved.shape[1]
    j_irrep = lax.dynamic_slice_in_dim(occ_irrep, lax.axis_index("red") * j_rows, j_rows, 0)
    out_irrep = jnp.bitwise_xor(occ_irrep[:, None], j_irrep[None, :])
    out = jnp.where(out_irrep[:, :, None, None] == label, moved, jnp.zeros((), BF16))
    return out.reshape(occupied, j_rows, width)


OWNERS = 8
REDS = 4
V_CHUNKS = 2


def place(offset):
    core, x, y, low, high = [(offset >> b) & 1 for b in range(5)]
    return ((((core ^ y ^ low ^ high) * 2 + x) * 2 + low) * 2 + y) * 2 + high


CORE, X, Y, LOW, HIGH = 0b00001, 0b00010, 0b00101, 0b01001, 0b10001


def pick(vectors, shift_bits):
    for b in range(3):
        vectors = [
            jnp.where(shift_bits[b], vectors[(d + 2**b) % 8], vectors[d]) for d in range(8)
        ]
    return vectors


def turn(vector, blocks):
    return pltpu.roll(vector, blocks % LABELS * BLOCK, 1) if blocks % LABELS else vector


def bits_of(labels):
    return [((labels >> b) & 1) == 1 for b in range(3)]


def sums_kernel(
    occ_hbm, vir_hbm, cd_hbm, t_hbm, v_hbm, sums, j_out, i_out,
    t_buf, v_buf, w_buf, total, occ, vir, cd, t_sem, v_sem, s_sem,
):
    rows, occupied, depth = t_buf.shape
    span = depth // V_CHUNKS
    small = [
        pltpu.make_async_copy(source, target, s_sem.at[n])
        for n, (source, target) in enumerate(((occ_hbm, occ), (vir_hbm, vir), (cd_hbm, cd)))
    ]
    v_copies = [
        pltpu.make_async_copy(
            v_hbm.at[pl.ds(c * span, span), :], v_buf.at[pl.ds(c * span, span), :], v_sem.at[c]
        )
        for c in range(V_CHUNKS)
    ]
    t_copy = pltpu.make_async_copy(t_hbm, t_buf, t_sem)
    for copy in (*small, *v_copies, t_copy):
        copy.start()
    pair, red = lax.axis_index("pair"), lax.axis_index("red")
    for copy in small:
        copy.wait()

    zero, one = jnp.zeros((), BF16), jnp.ones((), BF16)
    sublane = lax.broadcasted_iota(I32, (8, LANES), 0)
    lane_block = lax.broadcasted_iota(I32, (8, LANES), 1) // BLOCK

    def column(first):
        value = jnp.full((8, LANES), occ[first], I32)
        for s in range(1, 8):
            value = jnp.where(sublane == s, occ[first + s], value)
        return value

    occ_j = [column(8 * g) for g in range(occupied // 8)]
    occ_j16 = jnp.concatenate(occ_j, 0).astype(F32).astype(BF16)
    occ_i = [occ[pair * rows + i] for i in range(rows)]

    j_rows = occupied // REDS
    for g in range(j_rows // 8):
        value = column(red * j_rows + 8 * g) ^ lane_block
        j_out[pl.ds(8 * g, 8), :] = value.astype(F32)
    for a in range(OWNERS):
        i_out[pl.ds(8 * a, 8), :] = column((pair ^ a) * rows).astype(F32)

    pieces = vir.shape[0] // LANES
    table = [
        jnp.broadcast_to(vir[pl.ds(LANES * n, LANES)].reshape(1, LANES), (8, LANES))
        for n in range(pieces)
    ]
    block_row = (lax.broadcasted_iota(I32, (LANES, LANES), 0) // BLOCK).astype(F32).astype(BF16)
    labels, masks = [], []
    for q in range(depth // LANES):
        index = cd[:, pl.ds(q * LANES, LANES)]
        index = jnp.concatenate([index, jnp.zeros((6, LANES), I32)], 0)
        within, piece = index % LANES, index // LANES
        found = jnp.take_along_axis(table[0], within, axis=1)
        for n in range(1, pieces):
            found = jnp.where(piece == n, jnp.take_along_axis(table[n], within, axis=1), found)
        label = found[0:1] ^ found[1:2]
        labels.append(label)
        spread = jnp.broadcast_to(label, (LANES, LANES)).astype(F32).astype(BF16)
        masks.append(jnp.where(spread == block_row, one, zero).T)

    for c in range(V_CHUNKS):
        v_copies[c].wait()
        for q in range(c * span // LANES, (c + 1) * span // LANES):
            ks = pl.ds(q * LANES, LANES)
            mask = masks[q] != zero
            folded = jnp.where(mask, v_buf[ks, 0:LANES], zero)
            for p in range(1, OWNERS):
                part = jnp.where(mask, v_buf[ks, pl.ds(p * LANES, LANES)], zero)
                folded = folded + turn(part, p)
            w_buf[ks, :] = folded

    t_copy.wait()
    masked = []
    for i in range(rows):
        row = []
        for q in range(depth // LANES):
            wanted = jnp.broadcast_to(labels[q] ^ occ_i[i], (occupied, LANES))
            wanted = wanted.astype(F32).astype(BF16)
            row.append(jnp.where(wanted == occ_j16, t_buf[i, :, pl.ds(q * LANES, LANES)], zero))
        masked.append(jnp.concatenate(row, 1))
    total[...] = jnp.dot(
        jnp.concatenate(masked, 0), w_buf[...], preferred_element_type=F32
    )

    lane_bits = bits_of(lane_block)
    occ_i_lane = jnp.zeros((8, LANES), I32)
    for i in range(rows):
        occ_i_lane = jnp.where(lane_block == i, occ_i[i], occ_i_lane)
    me = pair * REDS + red
    for g in range(occupied // 8):
        held = [turn(total[pl.ds(i * occupied + g * 8, 8), :], i) for i in range(rows)]
        skewed = pick(held, lane_bits)
        held = [turn(skewed[-d % 8], -d) for d in range(8)]
        held = pick(held, bits_of(occ_j[g] ^ occ_i_lane))
        for p in range(OWNERS):
            to = place((p * REDS + g * 8 // j_rows) ^ me)
            sums[to, pl.ds(g * 8 % j_rows, 8), :] = held[p]


def spread_kernel(offsets, j_in, i_in, *refs):
    arrays, (out, buf, sem) = refs[: len(offsets)], refs[-3:]
    pair = lax.axis_index("pair")
    j_side = j_in[...].astype(BF16)
    bits = bits_of(lax.broadcasted_iota(I32, j_side.shape, 1) // BLOCK)
    sources = [(ref, k, a) for ref, of in zip(arrays, offsets) for k, a in enumerate(of)]
    copies = []
    for n, (ref, k, a) in enumerate(sources):
        level = [ref[k]]
        for b in (2, 1, 0):
            level = [
                jnp.where(bits[b], *((v, turn(v, -(2**b))) if upper else (turn(v, 2**b), v)))
                for v in level
                for upper in (False, True)
            ]
        for i in range(8):
            wanted = jnp.broadcast_to(i_in[pl.ds(8 * a + i, 1), :], j_side.shape).astype(BF16)
            buf[n, i] = jnp.where(wanted == j_side, level[i], jnp.zeros((), BF16))
        copy = pltpu.make_async_copy(buf.at[n], out.at[pl.ds((pair ^ a) * 8, 8)], sem.at[n])
        copy.start()
        copies.append(copy)
    for copy in copies:
        copy.wait()


def spread(j_side, i_side, blocks, so_far=None):
    offsets, arrays = [of for of, _ in blocks], [array for _, array in blocks]
    count = sum(len(of) for of in offsets)
    occupied, j_rows = i_side.shape[0], j_side.shape[0]
    vmem, hbm = pl.BlockSpec(memory_space=pltpu.VMEM), pl.BlockSpec(memory_space=pltpu.HBM)
    earlier = [] if so_far is None else [so_far]
    return pl.pallas_call(
        functools.partial(spread_kernel, offsets),
        out_shape=jax.ShapeDtypeStruct((occupied, j_rows, LANES), BF16),
        in_specs=[vmem] * (2 + len(arrays)) + [hbm] * len(earlier),
        out_specs=hbm,
        scratch_shapes=[
            pltpu.VMEM((count, 8, j_rows, LANES), BF16),
            pltpu.SemaphoreType.DMA((count,)),
        ],
        input_output_aliases={2 + len(arrays): 0} if earlier else {},
        compiler_params=pltpu.CompilerParams(vmem_limit_bytes=8 * 2**20),
        cost_estimate=pl.CostEstimate(
            flops=10**6, bytes_accessed=2 * count * 8 * j_rows * LANES, transcendentals=0
        ),
        name="spread",
    )(j_side, i_side, *arrays, *earlier)


def in_hbm(*arrays):
    return [pltpu.with_memory_space_constraint(a, pltpu.HBM) for a in arrays]


def fast(amplitudes, integrals, occ_irrep, vir_irrep, cd_orbitals, ab_orbitals):
    rows, occupied, depth = amplitudes.shape
    j_rows = occupied // REDS
    vmem, hbm = pl.BlockSpec(memory_space=pltpu.VMEM), pl.BlockSpec(memory_space=pltpu.HBM)
    sums, j_side, i_side = pl.pallas_call(
        sums_kernel,
        out_shape=(
            jax.ShapeDtypeStruct((OWNERS * REDS, j_rows, LANES), F32),
            jax.ShapeDtypeStruct((j_rows, LANES), F32),
            jax.ShapeDtypeStruct((occupied, LANES), F32),
        ),
        in_specs=[hbm] * 5,
        out_specs=(vmem,) * 3,
        scratch_shapes=[
            pltpu.VMEM(amplitudes.shape, BF16),
            pltpu.VMEM(integrals.shape, BF16),
            pltpu.VMEM((depth, LANES), BF16),
            pltpu.VMEM((rows * occupied, LANES), F32),
            pltpu.SMEM(occ_irrep.shape, I32),
            pltpu.VMEM(vir_irrep.shape, I32),
            pltpu.VMEM(cd_orbitals.shape, I32),
            pltpu.SemaphoreType.DMA,
            pltpu.SemaphoreType.DMA((V_CHUNKS,)),
            pltpu.SemaphoreType.DMA((3,)),
        ],
        compiler_params=pltpu.CompilerParams(vmem_limit_bytes=32 * 2**20),
        name="sums",
    )(*in_hbm(occ_irrep, vir_irrep, cd_orbitals, amplitudes, integrals))

    def swap(block, pattern):
        pairs = [(d, d ^ pattern) for d in range(OWNERS * REDS)]
        return lax.ppermute(block, ("pair", "red"), pairs)

    shape = (2, 2, 2, 2, 2, j_rows, LANES)
    sums = sums.reshape(shape)
    chip = sums[0] + swap(sums[1], CORE)
    low = swap(chip[0, 1], LOW)
    across = swap(chip[1, 0], X)
    corner = swap(chip[1, 1], X ^ LOW)
    done = jnp.stack([(chip[0, 0] + across).astype(BF16), (low + corner).astype(BF16)])
    both = jnp.stack([done[:, 0], swap(done[:, 1], Y)]).reshape(4, 2, j_rows, LANES)
    high = swap(both[:, 1], HIGH)
    out = spread(j_side, i_side, [((0, 2, 1, 3), both[:, 0])])
    return spread(j_side, i_side, [((4, 6, 5, 7), high)], out)


def solution(mesh):
    def local(amplitudes, integrals, occ_irrep, vir_irrep, cd_orbitals, ab_orbitals):
        sizes = mesh.shape["pair"], mesh.shape["red"], amplitudes.shape[0], ab_orbitals.shape[1]
        form = fast if sizes == (OWNERS, REDS, 8, LANES) else general
        return form(amplitudes, integrals, occ_irrep, vir_irrep, cd_orbitals, ab_orbitals)

    in_specs = (P("pair", None, "red"), P("red", None), P(), P(), P(None, "red"), P(None, "pair"))
    out_specs = P(None, "red", "pair")
    return jax.shard_map(local, mesh=mesh, in_specs=in_specs, out_specs=out_specs, check_vma=False)
```

```python
import functools

import jax
import jax.numpy as jnp
from jax import lax
from jax.experimental import pallas as pl
from jax.experimental.pallas import tpu as pltpu
from jax.sharding import PartitionSpec as P

LABELS = 8
LANES = 128
BLOCK = LANES // LABELS
F32, BF16, I32 = jnp.float32, jnp.bfloat16, jnp.int32


def pair_labels(orbitals, vir_irrep):
    labels = lax.broadcasted_iota(I32, (1, vir_irrep.shape[0]), 1)
    first = jnp.sum(jnp.where(orbitals[0][:, None] == labels, vir_irrep[None, :], 0), axis=1)
    second = jnp.sum(jnp.where(orbitals[1][:, None] == labels, vir_irrep[None, :], 0), axis=1)
    return jnp.bitwise_xor(first, second)


def general(amplitudes, integrals, occ_irrep, vir_irrep, cd_orbitals, ab_orbitals):
    own_rows, occupied, depth = amplitudes.shape
    width = ab_orbitals.shape[1]
    owners = integrals.shape[1] // width
    block = width // LABELS
    own_irrep = lax.dynamic_slice_in_dim(occ_irrep, lax.axis_index("pair") * own_rows, own_rows, 0)
    pair_irrep = jnp.bitwise_xor(own_irrep[:, None], occ_irrep[None, :])
    cd_irrep = pair_labels(cd_orbitals, vir_irrep)
    masked = jnp.where(pair_irrep[:, :, None] == cd_irrep, amplitudes, jnp.zeros((), BF16))
    sums = jnp.dot(
        masked.reshape(own_rows * occupied, depth), integrals, preferred_element_type=F32
    ).reshape(own_rows, occupied, owners, LABELS, block)
    label = lax.broadcasted_iota(I32, (LABELS, 1), 0)
    kept = jnp.where(pair_irrep[:, :, None, None, None] == label, sums, 0.0).sum(axis=3)
    summed = lax.psum_scatter(kept, "red", scatter_dimension=1, tiled=True)
    moved = lax.all_to_all(
        summed.astype(BF16), "pair", split_axis=2, concat_axis=0, tiled=True
    )[:, :, 0, None, :]
    j_rows = moved.shape[1]
    j_irrep = lax.dynamic_slice_in_dim(occ_irrep, lax.axis_index("red") * j_rows, j_rows, 0)
    out_irrep = jnp.bitwise_xor(occ_irrep[:, None], j_irrep[None, :])
    out = jnp.where(out_irrep[:, :, None, None] == label, moved, jnp.zeros((), BF16))
    return out.reshape(occupied, j_rows, width)


OWNERS = 8
REDS = 4
V_CHUNKS = 2
BY_PRODUCT = 2


def place(offset):
    core, x, y, low, high = [(offset >> b) & 1 for b in range(5)]
    return ((((core ^ y ^ low ^ high) * 2 + x) * 2 + low) * 2 + y) * 2 + high


CORE, X, Y, LOW, HIGH = 0b00001, 0b00010, 0b00101, 0b01001, 0b10001


def pick(vectors, shift_bits):
    for b in range(3):
        vectors = [
            jnp.where(shift_bits[b], vectors[(d + 2**b) % 8], vectors[d]) for d in range(8)
        ]
    return vectors


def turn(vector, blocks):
    return pltpu.roll(vector, blocks % LABELS * BLOCK, 1) if blocks % LABELS else vector


def bits_of(labels):
    return [((labels >> b) & 1) == 1 for b in range(3)]


def sums_kernel(
    occ_hbm, vir_hbm, cd_hbm, t_hbm, v_hbm, sums, j_out, i_out,
    t_buf, v_buf, w_buf, total, occ, vir, cd, t_sem, v_sem, s_sem,
):
    rows, occupied, depth = t_buf.shape
    span = depth // V_CHUNKS
    small = [
        pltpu.make_async_copy(source, target, s_sem.at[n])
        for n, (source, target) in enumerate(((occ_hbm, occ), (vir_hbm, vir), (cd_hbm, cd)))
    ]
    v_copies = [
        pltpu.make_async_copy(
            v_hbm.at[pl.ds(c * span, span), :], v_buf.at[pl.ds(c * span, span), :], v_sem.at[c]
        )
        for c in range(V_CHUNKS)
    ]
    t_copy = pltpu.make_async_copy(t_hbm, t_buf, t_sem)
    for copy in (*small, *v_copies, t_copy):
        copy.start()
    pair, red = lax.axis_index("pair"), lax.axis_index("red")
    for copy in small:
        copy.wait()

    zero, one = jnp.zeros((), BF16), jnp.ones((), BF16)
    sublane = lax.broadcasted_iota(I32, (8, LANES), 0)
    lane_block = lax.broadcasted_iota(I32, (8, LANES), 1) // BLOCK

    def column(first):
        value = jnp.full((8, LANES), occ[first], I32)
        for s in range(1, 8):
            value = jnp.where(sublane == s, occ[first + s], value)
        return value

    occ_j = [column(8 * g) for g in range(occupied // 8)]
    occ_i = [occ[pair * rows + i] for i in range(rows)]

    j_rows = occupied // REDS
    for g in range(j_rows // 8):
        value = column(red * j_rows + 8 * g) ^ lane_block
        j_out[pl.ds(8 * g, 8), :] = value.astype(F32)
    for a in range(OWNERS):
        i_out[pl.ds(8 * a, 8), :] = column((pair ^ a) * rows).astype(F32)

    pieces = vir.shape[0] // LANES
    table = [
        jnp.broadcast_to(vir[pl.ds(LANES * n, LANES)].reshape(1, LANES), (8, LANES))
        for n in range(pieces)
    ]
    sub_block = lax.broadcasted_iota(I32, (BLOCK, LANES), 0) // BLOCK
    block_rows = [(sub_block + b).astype(F32).astype(BF16) for b in range(LABELS)]
    labels, masks = [], []
    for z in range(depth // LANES // 4):
        index = jnp.concatenate([cd[:, pl.ds((4 * z + u) * LANES, LANES)] for u in range(4)], 0)
        within, piece = index % LANES, index // LANES
        found = jnp.take_along_axis(table[0], within, axis=1)
        for n in range(1, pieces):
            found = jnp.where(piece == n, jnp.take_along_axis(table[n], within, axis=1), found)
        found = (found ^ pltpu.roll(found, 7, 0)).astype(F32)
        for u in range(4):
            label = jnp.broadcast_to(found[2 * u : 2 * u + 1], (BLOCK, LANES)).astype(BF16)
            labels.append(label)
            own = [jnp.where(label == row, one, zero) for row in block_rows]
            masks.append(jnp.concatenate(own, 0).T)
    own_labels = [
        [
            (jnp.concatenate(occ_j[g : g + 2], 0) ^ occ_i[i]).astype(F32).astype(BF16)
            for g in range(0, occupied // 8, 2)
        ]
        for i in range(rows)
    ]

    turned = OWNERS - BY_PRODUCT
    row = lax.broadcasted_iota(I32, (BY_PRODUCT * LANES, LANES), 0)
    lane = lax.broadcasted_iota(I32, (BY_PRODUCT * LANES, LANES), 1)
    target = (row + (row // LANES + turned) * BLOCK) % LANES
    permutation = jnp.where(target == lane, 1.0, 0.0).astype(BF16)
    for c in range(V_CHUNKS):
        v_copies[c].wait()
        for q in range(c * span // LANES, (c + 1) * span // LANES):
            ks = pl.ds(q * LANES, LANES)
            parts = [masks[q] * v_buf[ks, pl.ds(p * LANES, LANES)] for p in range(OWNERS)]
            folded = parts[0]
            for p in range(1, turned):
                folded = folded + turn(parts[p], p)
            rest = jnp.concatenate(parts[turned:], 1)
            rest = jnp.dot(rest, permutation, preferred_element_type=F32).astype(BF16)
            w_buf[ks, :] = folded + rest

    t_copy.wait()
    masked = []
    for i in range(rows):
        row = []
        for q in range(depth // LANES):
            group = t_buf[i, :, pl.ds(q * LANES, LANES)]
            kept = [
                jnp.where(labels[q] == own, group[g * BLOCK : (g + 1) * BLOCK], zero)
                for g, own in enumerate(own_labels[i])
            ]
            row.append(jnp.concatenate(kept, 0))
        masked.append(jnp.concatenate(row, 1))
    total[...] = jnp.dot(
        jnp.concatenate(masked, 0), w_buf[...], preferred_element_type=F32
    )

    lane_bits = bits_of(lane_block)
    occ_i_lane = jnp.zeros((8, LANES), I32)
    for i in range(rows):
        occ_i_lane = jnp.where(lane_block == i, occ_i[i], occ_i_lane)
    me = pair * REDS + red
    for g in range(occupied // 8):
        held = [turn(total[pl.ds(i * occupied + g * 8, 8), :], i) for i in range(rows)]
        skewed = pick(held, lane_bits)
        held = [turn(skewed[-d % 8], -d) for d in range(8)]
        held = pick(held, bits_of(occ_j[g] ^ occ_i_lane))
        for p in range(OWNERS):
            to = place((p * REDS + g * 8 // j_rows) ^ me)
            sums[to, pl.ds(g * 8 % j_rows, 8), :] = held[p]


def spread_kernel(offsets, j_in, i_in, *refs):
    arrays, (out, buf, sem) = refs[: len(offsets)], refs[-3:]
    pair = lax.axis_index("pair")
    j_side = j_in[...].astype(BF16)
    bits = bits_of(lax.broadcasted_iota(I32, j_side.shape, 1) // BLOCK)
    sources = [(ref, k, a) for ref, of in zip(arrays, offsets) for k, a in enumerate(of)]
    copies = []
    for n, (ref, k, a) in enumerate(sources):
        skewed = pick([turn(ref[k], d) for d in range(LABELS)], bits)
        for i in range(8):
            wanted = jnp.broadcast_to(i_in[pl.ds(8 * a + i, 1), :], j_side.shape).astype(BF16)
            buf[n, i] = jnp.where(wanted == j_side, skewed[-i % LABELS], jnp.zeros((), BF16))
        copy = pltpu.make_async_copy(buf.at[n], out.at[pl.ds((pair ^ a) * 8, 8)], sem.at[n])
        copy.start()
        copies.append(copy)
    for copy in copies:
        copy.wait()


def spread(j_side, i_side, blocks, so_far=None):
    offsets, arrays = [of for of, _ in blocks], [array for _, array in blocks]
    count = sum(len(of) for of in offsets)
    occupied, j_rows = i_side.shape[0], j_side.shape[0]
    vmem, hbm = pl.BlockSpec(memory_space=pltpu.VMEM), pl.BlockSpec(memory_space=pltpu.HBM)
    earlier = [] if so_far is None else [so_far]
    return pl.pallas_call(
        functools.partial(spread_kernel, offsets),
        out_shape=jax.ShapeDtypeStruct((occupied, j_rows, LANES), BF16),
        in_specs=[vmem] * (2 + len(arrays)) + [hbm] * len(earlier),
        out_specs=hbm,
        scratch_shapes=[
            pltpu.VMEM((count, 8, j_rows, LANES), BF16),
            pltpu.SemaphoreType.DMA((count,)),
        ],
        input_output_aliases={2 + len(arrays): 0} if earlier else {},
        compiler_params=pltpu.CompilerParams(vmem_limit_bytes=8 * 2**20),
        cost_estimate=pl.CostEstimate(
            flops=10**6, bytes_accessed=2 * count * 8 * j_rows * LANES, transcendentals=0
        ),
        name="spread",
    )(j_side, i_side, *arrays, *earlier)


def in_hbm(*arrays):
    return [pltpu.with_memory_space_constraint(a, pltpu.HBM) for a in arrays]


def fast(amplitudes, integrals, occ_irrep, vir_irrep, cd_orbitals, ab_orbitals):
    rows, occupied, depth = amplitudes.shape
    j_rows = occupied // REDS
    vmem, hbm = pl.BlockSpec(memory_space=pltpu.VMEM), pl.BlockSpec(memory_space=pltpu.HBM)
    sums, j_side, i_side = pl.pallas_call(
        sums_kernel,
        out_shape=(
            jax.ShapeDtypeStruct((OWNERS * REDS, j_rows, LANES), F32),
            jax.ShapeDtypeStruct((j_rows, LANES), F32),
            jax.ShapeDtypeStruct((occupied, LANES), F32),
        ),
        in_specs=[hbm] * 5,
        out_specs=(vmem,) * 3,
        scratch_shapes=[
            pltpu.VMEM(amplitudes.shape, BF16),
            pltpu.VMEM(integrals.shape, BF16),
            pltpu.VMEM((depth, LANES), BF16),
            pltpu.VMEM((rows * occupied, LANES), F32),
            pltpu.SMEM(occ_irrep.shape, I32),
            pltpu.VMEM(vir_irrep.shape, I32),
            pltpu.VMEM(cd_orbitals.shape, I32),
            pltpu.SemaphoreType.DMA,
            pltpu.SemaphoreType.DMA((V_CHUNKS,)),
            pltpu.SemaphoreType.DMA((3,)),
        ],
        compiler_params=pltpu.CompilerParams(vmem_limit_bytes=32 * 2**20),
        name="sums",
    )(*in_hbm(occ_irrep, vir_irrep, cd_orbitals, amplitudes, integrals))

    def swap(block, pattern):
        pairs = [(d, d ^ pattern) for d in range(OWNERS * REDS)]
        return lax.ppermute(block, ("pair", "red"), pairs)

    shape = (2, 2, 2, 2, 2, j_rows, LANES)
    sums = sums.reshape(shape)
    chip = sums[0] + swap(sums[1], CORE)
    low = swap(chip[0, 1], LOW)
    across = swap(chip[1, 0], X)
    corner = swap(chip[1, 1], X ^ LOW)
    done = jnp.stack([(chip[0, 0] + across).astype(BF16), (low + corner).astype(BF16)])
    both = jnp.stack([done[:, 0], swap(done[:, 1], Y)]).reshape(4, 2, j_rows, LANES)
    high = swap(both[:, 1], HIGH)
    out = spread(j_side, i_side, [((0, 2, 1, 3), both[:, 0])])
    return spread(j_side, i_side, [((4, 6, 5, 7), high)], out)


def solution(mesh):
    def local(amplitudes, integrals, occ_irrep, vir_irrep, cd_orbitals, ab_orbitals):
        sizes = mesh.shape["pair"], mesh.shape["red"], amplitudes.shape[0], ab_orbitals.shape[1]
        form = fast if sizes == (OWNERS, REDS, 8, LANES) else general
        return form(amplitudes, integrals, occ_irrep, vir_irrep, cd_orbitals, ab_orbitals)

    in_specs = (P("pair", None, "red"), P("red", None), P(), P(), P(None, "red"), P(None, "pair"))
    out_specs = P(None, "red", "pair")
    return jax.shard_map(local, mesh=mesh, in_specs=in_specs, out_specs=out_specs, check_vma=False)
```

```python
import functools

import jax
import jax.numpy as jnp
from jax import lax
from jax.experimental import pallas as pl
from jax.experimental.pallas import tpu as pltpu
from jax.sharding import PartitionSpec as P

LABELS = 8
LANES = 128
BLOCK = LANES // LABELS
F32, BF16, I32 = jnp.float32, jnp.bfloat16, jnp.int32


def pair_labels(orbitals, vir_irrep):
    labels = lax.broadcasted_iota(I32, (1, vir_irrep.shape[0]), 1)
    first = jnp.sum(jnp.where(orbitals[0][:, None] == labels, vir_irrep[None, :], 0), axis=1)
    second = jnp.sum(jnp.where(orbitals[1][:, None] == labels, vir_irrep[None, :], 0), axis=1)
    return jnp.bitwise_xor(first, second)


def general(amplitudes, integrals, occ_irrep, vir_irrep, cd_orbitals, ab_orbitals):
    own_rows, occupied, depth = amplitudes.shape
    width = ab_orbitals.shape[1]
    owners = integrals.shape[1] // width
    block = width // LABELS
    own_irrep = lax.dynamic_slice_in_dim(occ_irrep, lax.axis_index("pair") * own_rows, own_rows, 0)
    pair_irrep = jnp.bitwise_xor(own_irrep[:, None], occ_irrep[None, :])
    cd_irrep = pair_labels(cd_orbitals, vir_irrep)
    masked = jnp.where(pair_irrep[:, :, None] == cd_irrep, amplitudes, jnp.zeros((), BF16))
    sums = jnp.dot(
        masked.reshape(own_rows * occupied, depth), integrals, preferred_element_type=F32
    ).reshape(own_rows, occupied, owners, LABELS, block)
    label = lax.broadcasted_iota(I32, (LABELS, 1), 0)
    kept = jnp.where(pair_irrep[:, :, None, None, None] == label, sums, 0.0).sum(axis=3)
    summed = lax.psum_scatter(kept, "red", scatter_dimension=1, tiled=True)
    moved = lax.all_to_all(
        summed.astype(BF16), "pair", split_axis=2, concat_axis=0, tiled=True
    )[:, :, 0, None, :]
    j_rows = moved.shape[1]
    j_irrep = lax.dynamic_slice_in_dim(occ_irrep, lax.axis_index("red") * j_rows, j_rows, 0)
    out_irrep = jnp.bitwise_xor(occ_irrep[:, None], j_irrep[None, :])
    out = jnp.where(out_irrep[:, :, None, None] == label, moved, jnp.zeros((), BF16))
    return out.reshape(occupied, j_rows, width)


OWNERS = 8
REDS = 4
V_CHUNKS = 2
BY_PRODUCT = 2


def place(offset):
    core, x, y, low, high = [(offset >> b) & 1 for b in range(5)]
    return ((((core ^ y ^ low ^ high) * 2 + x) * 2 + low) * 2 + y) * 2 + high


CORE, X, Y, LOW, HIGH = 0b00001, 0b00010, 0b00101, 0b01001, 0b10001


def pick(vectors, shift_bits):
    for b in range(3):
        vectors = [
            jnp.where(shift_bits[b], vectors[(d + 2**b) % 8], vectors[d]) for d in range(8)
        ]
    return vectors


def turn(vector, blocks):
    return pltpu.roll(vector, blocks % LABELS * BLOCK, 1) if blocks % LABELS else vector


def bits_of(labels):
    return [((labels >> b) & 1) == 1 for b in range(3)]


def sums_kernel(
    occ_hbm, vir_hbm, cd_hbm, t_hbm, v_hbm, sums, j_out, i_out,
    t_buf, v_buf, w_buf, total, occ, vir, cd, t_sem, v_sem, s_sem,
):
    rows, occupied, depth = t_buf.shape
    span = depth // V_CHUNKS
    small = [
        pltpu.make_async_copy(source, target, s_sem.at[n])
        for n, (source, target) in enumerate(((occ_hbm, occ), (vir_hbm, vir), (cd_hbm, cd)))
    ]
    v_copies = [
        pltpu.make_async_copy(
            v_hbm.at[pl.ds(c * span, span), :], v_buf.at[pl.ds(c * span, span), :], v_sem.at[c]
        )
        for c in range(V_CHUNKS)
    ]
    t_copy = pltpu.make_async_copy(t_hbm, t_buf, t_sem)
    for copy in (*small, *v_copies, t_copy):
        copy.start()
    pair, red = lax.axis_index("pair"), lax.axis_index("red")
    for copy in small:
        copy.wait()

    zero, one = jnp.zeros((), BF16), jnp.ones((), BF16)
    sublane = lax.broadcasted_iota(I32, (8, LANES), 0)
    lane_block = lax.broadcasted_iota(I32, (8, LANES), 1) // BLOCK

    def column(first):
        value = jnp.full((8, LANES), occ[first], I32)
        for s in range(1, 8):
            value = jnp.where(sublane == s, occ[first + s], value)
        return value

    occ_j = [column(8 * g) for g in range(occupied // 8)]
    occ_i = [occ[pair * rows + i] for i in range(rows)]

    j_rows = occupied // REDS
    for g in range(j_rows // 8):
        value = column(red * j_rows + 8 * g) ^ lane_block
        j_out[pl.ds(8 * g, 8), :] = value.astype(F32)
    for a in range(OWNERS):
        i_out[pl.ds(8 * a, 8), :] = column((pair ^ a) * rows).astype(F32)

    pieces = vir.shape[0] // LANES
    table = [
        jnp.broadcast_to(vir[pl.ds(LANES * n, LANES)].reshape(1, LANES), (8, LANES))
        for n in range(pieces)
    ]
    sub_block = lax.broadcasted_iota(I32, (BLOCK, LANES), 0) // BLOCK
    block_rows = [(sub_block + b).astype(F32).astype(BF16) for b in range(LABELS)]
    labels, masks = [], []
    for z in range(depth // LANES // 4):
        index = jnp.concatenate([cd[:, pl.ds((4 * z + u) * LANES, LANES)] for u in range(4)], 0)
        within, piece = index % LANES, index // LANES
        found = jnp.take_along_axis(table[0], within, axis=1)
        for n in range(1, pieces):
            found = jnp.where(piece == n, jnp.take_along_axis(table[n], within, axis=1), found)
        found = (found ^ pltpu.roll(found, 7, 0)).astype(F32)
        for u in range(4):
            label = jnp.broadcast_to(found[2 * u : 2 * u + 1], (BLOCK, LANES)).astype(BF16)
            labels.append(label)
            own = [jnp.where(label == row, one, zero) for row in block_rows]
            masks.append(jnp.concatenate(own, 0).T)
    own_labels = [
        [
            (jnp.concatenate(occ_j[g : g + 2], 0) ^ occ_i[i]).astype(F32).astype(BF16)
            for g in range(0, occupied // 8, 2)
        ]
        for i in range(rows)
    ]

    turned = OWNERS - BY_PRODUCT
    row = lax.broadcasted_iota(I32, (BY_PRODUCT * LANES, LANES), 0)
    lane = lax.broadcasted_iota(I32, (BY_PRODUCT * LANES, LANES), 1)
    target = (row + (row // LANES + turned) * BLOCK) % LANES
    permutation = jnp.where(target == lane, 1.0, 0.0).astype(BF16)
    for c in range(V_CHUNKS):
        v_copies[c].wait()
        for q in range(c * span // LANES, (c + 1) * span // LANES):
            ks = pl.ds(q * LANES, LANES)
            parts = [masks[q] * v_buf[ks, pl.ds(p * LANES, LANES)] for p in range(OWNERS)]
            folded = parts[0]
            for p in range(1, turned):
                folded = folded + turn(parts[p], p)
            rest = jnp.concatenate(parts[turned:], 1)
            rest = jnp.dot(rest, permutation, preferred_element_type=F32).astype(BF16)
            w_buf[ks, :] = folded + rest

    t_copy.wait()
    masked = []
    for i in range(rows):
        row = []
        for q in range(depth // LANES):
            group = t_buf[i, :, pl.ds(q * LANES, LANES)]
            kept = [
                jnp.where(labels[q] == own, group[g * BLOCK : (g + 1) * BLOCK], zero)
                for g, own in enumerate(own_labels[i])
            ]
            row.append(jnp.concatenate(kept, 0))
        masked.append(jnp.concatenate(row, 1))
    total[...] = jnp.dot(
        jnp.concatenate(masked, 0), w_buf[...], preferred_element_type=F32
    )

    lane_bits = bits_of(lane_block)
    occ_i_lane = jnp.zeros((8, LANES), I32)
    for i in range(rows):
        occ_i_lane = jnp.where(lane_block == i, occ_i[i], occ_i_lane)
    me = pair * REDS + red
    for g in range(occupied // 8):
        held = [turn(total[pl.ds(i * occupied + g * 8, 8), :], i) for i in range(rows)]
        skewed = pick(held, lane_bits)
        held = [turn(skewed[-d % 8], -d) for d in range(8)]
        held = pick(held, bits_of(occ_j[g] ^ occ_i_lane))
        for p in range(OWNERS):
            to = place((p * REDS + g * 8 // j_rows) ^ me)
            sums[to, pl.ds(g * 8 % j_rows, 8), :] = held[p]


def turned_blocks(block, bits):
    skewed = pick([turn(block, d) for d in range(LABELS)], bits)
    return [skewed[-i % LABELS] for i in range(LABELS)]


def send_rows(blocks, offsets, masks, out, buf, sem):
    pair = lax.axis_index("pair")
    bits = bits_of(lax.broadcasted_iota(I32, blocks.shape[1:], 1) // BLOCK)
    for n, a in enumerate(offsets):
        for i, block in enumerate(turned_blocks(blocks[n], bits)):
            buf[n, i] = block * masks(n, i)
        rows = out.at[pl.ds((pair ^ a) * 8, 8)]
        pltpu.make_async_copy(buf.at[n], rows, sem).start()
    return pltpu.make_async_copy(buf, buf, sem)


def first_kernel(offsets, later, blocks, j_in, i_in, out, later_masks, buf, sem):
    j_side = j_in[...].astype(BF16)

    def mask(a, i):
        wanted = jnp.broadcast_to(i_in[pl.ds(8 * a + i, 1), :], j_side.shape).astype(BF16)
        return jnp.where(wanted == j_side, jnp.ones((), BF16), jnp.zeros((), BF16))

    all_rows = send_rows(blocks, offsets, lambda n, i: mask(offsets[n], i), out, buf, sem)
    for n, a in enumerate(later):
        for i in range(8):
            later_masks[n, i] = mask(a, i)
    all_rows.wait()


def last_kernel(offsets, blocks, masks, so_far, out, buf, sem):
    send_rows(blocks, offsets, lambda n, i: masks[n, i], out, buf, sem).wait()


def spread(kernel, operands, in_specs, out_shape, out_specs, shape, **more):
    return pl.pallas_call(
        kernel,
        out_shape=out_shape,
        in_specs=in_specs,
        out_specs=out_specs,
        scratch_shapes=[pltpu.VMEM(shape, BF16), pltpu.SemaphoreType.DMA],
        compiler_params=pltpu.CompilerParams(vmem_limit_bytes=8 * 2**20),
        cost_estimate=pl.CostEstimate(flops=10**6, bytes_accessed=2**18, transcendentals=0),
        name="spread",
        **more,
    )(*operands)


def in_hbm(*arrays):
    return [pltpu.with_memory_space_constraint(a, pltpu.HBM) for a in arrays]


def fast(amplitudes, integrals, occ_irrep, vir_irrep, cd_orbitals, ab_orbitals):
    rows, occupied, depth = amplitudes.shape
    j_rows = occupied // REDS
    vmem, hbm = pl.BlockSpec(memory_space=pltpu.VMEM), pl.BlockSpec(memory_space=pltpu.HBM)
    sums, j_side, i_side = pl.pallas_call(
        sums_kernel,
        out_shape=(
            jax.ShapeDtypeStruct((OWNERS * REDS, j_rows, LANES), F32),
            jax.ShapeDtypeStruct((j_rows, LANES), F32),
            jax.ShapeDtypeStruct((occupied, LANES), F32),
        ),
        in_specs=[hbm] * 5,
        out_specs=(vmem,) * 3,
        scratch_shapes=[
            pltpu.VMEM(amplitudes.shape, BF16),
            pltpu.VMEM(integrals.shape, BF16),
            pltpu.VMEM((depth, LANES), BF16),
            pltpu.VMEM((rows * occupied, LANES), F32),
            pltpu.SMEM(occ_irrep.shape, I32),
            pltpu.VMEM(vir_irrep.shape, I32),
            pltpu.VMEM(cd_orbitals.shape, I32),
            pltpu.SemaphoreType.DMA,
            pltpu.SemaphoreType.DMA((V_CHUNKS,)),
            pltpu.SemaphoreType.DMA((3,)),
        ],
        compiler_params=pltpu.CompilerParams(vmem_limit_bytes=32 * 2**20),
        name="sums",
    )(*in_hbm(occ_irrep, vir_irrep, cd_orbitals, amplitudes, integrals))

    def swap(block, pattern):
        pairs = [(d, d ^ pattern) for d in range(OWNERS * REDS)]
        return lax.ppermute(block, ("pair", "red"), pairs)

    shape = (2, 2, 2, 2, 2, j_rows, LANES)
    sums = sums.reshape(shape)
    chip = sums[0] + swap(sums[1], CORE)
    low = swap(chip[0, 1], LOW)
    across = swap(chip[1, 0], X)
    corner = swap(chip[1, 1], X ^ LOW)
    done = jnp.stack([(chip[0, 0] + across).astype(BF16), (low + corner).astype(BF16)])
    both = jnp.stack([done[:, 0], swap(done[:, 1], Y)]).reshape(4, 2, j_rows, LANES)
    high = swap(both[:, 1], HIGH)
    shape = (4, 8, j_rows, LANES)
    result = jax.ShapeDtypeStruct((occupied, j_rows, LANES), BF16)
    near, far = (0, 2, 1, 3), (4, 6, 5, 7)
    out, masks = spread(
        functools.partial(first_kernel, near, far), (both[:, 0], j_side, i_side), [vmem] * 3,
        (result, jax.ShapeDtypeStruct(shape, BF16)), (hbm, vmem), shape,
    )
    return spread(
        functools.partial(last_kernel, far), (high, masks, out), [vmem, vmem, hbm],
        result, hbm, shape, input_output_aliases={2: 0},
    )


def solution(mesh):
    def local(amplitudes, integrals, occ_irrep, vir_irrep, cd_orbitals, ab_orbitals):
        sizes = mesh.shape["pair"], mesh.shape["red"], amplitudes.shape[0], ab_orbitals.shape[1]
        form = fast if sizes == (OWNERS, REDS, 8, LANES) else general
        return form(amplitudes, integrals, occ_irrep, vir_irrep, cd_orbitals, ab_orbitals)

    in_specs = (P("pair", None, "red"), P("red", None), P(), P(), P(None, "red"), P(None, "pair"))
    out_specs = P(None, "red", "pair")
    return jax.shard_map(local, mesh=mesh, in_specs=in_specs, out_specs=out_specs, check_vma=False)
```

```python
import functools

import jax
import jax.numpy as jnp
from jax import lax
from jax.experimental import pallas as pl
from jax.experimental.pallas import tpu as pltpu
from jax.sharding import PartitionSpec as P

LABELS = 8
LANES = 128
BLOCK = LANES // LABELS
F32, BF16, I32 = jnp.float32, jnp.bfloat16, jnp.int32


def pair_labels(orbitals, vir_irrep):
    labels = lax.broadcasted_iota(I32, (1, vir_irrep.shape[0]), 1)
    first = jnp.sum(jnp.where(orbitals[0][:, None] == labels, vir_irrep[None, :], 0), axis=1)
    second = jnp.sum(jnp.where(orbitals[1][:, None] == labels, vir_irrep[None, :], 0), axis=1)
    return jnp.bitwise_xor(first, second)


def general(amplitudes, integrals, occ_irrep, vir_irrep, cd_orbitals, ab_orbitals):
    own_rows, occupied, depth = amplitudes.shape
    width = ab_orbitals.shape[1]
    owners = integrals.shape[1] // width
    block = width // LABELS
    own_irrep = lax.dynamic_slice_in_dim(occ_irrep, lax.axis_index("pair") * own_rows, own_rows, 0)
    pair_irrep = jnp.bitwise_xor(own_irrep[:, None], occ_irrep[None, :])
    cd_irrep = pair_labels(cd_orbitals, vir_irrep)
    masked = jnp.where(pair_irrep[:, :, None] == cd_irrep, amplitudes, jnp.zeros((), BF16))
    sums = jnp.dot(
        masked.reshape(own_rows * occupied, depth), integrals, preferred_element_type=F32
    ).reshape(own_rows, occupied, owners, LABELS, block)
    label = lax.broadcasted_iota(I32, (LABELS, 1), 0)
    kept = jnp.where(pair_irrep[:, :, None, None, None] == label, sums, 0.0).sum(axis=3)
    summed = lax.psum_scatter(kept, "red", scatter_dimension=1, tiled=True)
    moved = lax.all_to_all(
        summed.astype(BF16), "pair", split_axis=2, concat_axis=0, tiled=True
    )[:, :, 0, None, :]
    j_rows = moved.shape[1]
    j_irrep = lax.dynamic_slice_in_dim(occ_irrep, lax.axis_index("red") * j_rows, j_rows, 0)
    out_irrep = jnp.bitwise_xor(occ_irrep[:, None], j_irrep[None, :])
    out = jnp.where(out_irrep[:, :, None, None] == label, moved, jnp.zeros((), BF16))
    return out.reshape(occupied, j_rows, width)


OWNERS = 8
REDS = 4
V_CHUNKS = 2
BY_PRODUCT = 2


def place(offset):
    core, x, y, low, high = [(offset >> b) & 1 for b in range(5)]
    return ((((core ^ y ^ low ^ high) * 2 + x) * 2 + low) * 2 + y) * 2 + high


CORE, X, Y, LOW, HIGH = 0b00001, 0b00010, 0b00101, 0b01001, 0b10001


def pick(vectors, shift_bits):
    for b in range(3):
        vectors = [
            jnp.where(shift_bits[b], vectors[(d + 2**b) % 8], vectors[d]) for d in range(8)
        ]
    return vectors


def turn(vector, blocks):
    return pltpu.roll(vector, blocks % LABELS * BLOCK, 1) if blocks % LABELS else vector


def bits_of(labels):
    return [((labels >> b) & 1) == 1 for b in range(3)]


def sums_kernel(
    occ_hbm, vir_hbm, cd_hbm, t_hbm, v_hbm, sums, j_out, i_out,
    t_buf, v_buf, w_buf, total, occ, vir, cd, t_sem, v_sem, s_sem,
):
    rows, occupied, depth = t_buf.shape
    span = depth // V_CHUNKS
    small = [
        pltpu.make_async_copy(source, target, s_sem.at[n])
        for n, (source, target) in enumerate(((occ_hbm, occ), (vir_hbm, vir), (cd_hbm, cd)))
    ]
    v_copies = [
        pltpu.make_async_copy(
            v_hbm.at[pl.ds(c * span, span), :], v_buf.at[pl.ds(c * span, span), :], v_sem.at[c]
        )
        for c in range(V_CHUNKS)
    ]
    t_copy = pltpu.make_async_copy(t_hbm, t_buf, t_sem)
    for copy in (*small, *v_copies, t_copy):
        copy.start()
    pair, red = lax.axis_index("pair"), lax.axis_index("red")
    for copy in small:
        copy.wait()

    zero, one = jnp.zeros((), BF16), jnp.ones((), BF16)
    sublane = lax.broadcasted_iota(I32, (8, LANES), 0)
    lane_block = lax.broadcasted_iota(I32, (8, LANES), 1) // BLOCK

    def column(first):
        value = jnp.full((8, LANES), occ[first], I32)
        for s in range(1, 8):
            value = jnp.where(sublane == s, occ[first + s], value)
        return value

    occ_j = [column(8 * g) for g in range(occupied // 8)]
    occ_i = [occ[pair * rows + i] for i in range(rows)]

    j_rows = occupied // REDS
    for g in range(j_rows // 8):
        value = column(red * j_rows + 8 * g) ^ lane_block
        j_out[pl.ds(8 * g, 8), :] = value.astype(F32)
    for a in range(OWNERS):
        i_out[pl.ds(8 * a, 8), :] = column((pair ^ a) * rows).astype(F32)

    pieces = vir.shape[0] // LANES
    table = [
        jnp.broadcast_to(vir[pl.ds(LANES * n, LANES)].reshape(1, LANES), (8, LANES))
        for n in range(pieces)
    ]
    sub_block = lax.broadcasted_iota(I32, (BLOCK, LANES), 0) // BLOCK
    block_rows = [(sub_block + b).astype(F32).astype(BF16) for b in range(LABELS)]
    labels, masks = [], []
    for z in range(depth // LANES // 4):
        index = jnp.concatenate([cd[:, pl.ds((4 * z + u) * LANES, LANES)] for u in range(4)], 0)
        within, piece = index % LANES, index // LANES
        found = jnp.take_along_axis(table[0], within, axis=1)
        for n in range(1, pieces):
            found = jnp.where(piece == n, jnp.take_along_axis(table[n], within, axis=1), found)
        found = (found ^ pltpu.roll(found, 7, 0)).astype(F32)
        for u in range(4):
            label = jnp.broadcast_to(found[2 * u : 2 * u + 1], (BLOCK, LANES)).astype(BF16)
            labels.append(label)
            own = [jnp.where(label == row, one, zero) for row in block_rows]
            masks.append(jnp.concatenate(own, 0).T)
    own_labels = [
        [
            (jnp.concatenate(occ_j[g : g + 2], 0) ^ occ_i[i]).astype(F32).astype(BF16)
            for g in range(0, occupied // 8, 2)
        ]
        for i in range(rows)
    ]

    turned = OWNERS - BY_PRODUCT
    row = lax.broadcasted_iota(I32, (BY_PRODUCT * LANES, LANES), 0)
    lane = lax.broadcasted_iota(I32, (BY_PRODUCT * LANES, LANES), 1)
    target = (row + (row // LANES + turned) * BLOCK) % LANES
    permutation = jnp.where(target == lane, 1.0, 0.0).astype(BF16)
    for c in range(V_CHUNKS):
        v_copies[c].wait()
        for q in range(c * span // LANES, (c + 1) * span // LANES):
            ks = pl.ds(q * LANES, LANES)
            parts = [masks[q] * v_buf[ks, pl.ds(p * LANES, LANES)] for p in range(OWNERS)]
            folded = parts[0]
            for p in range(1, turned):
                folded = folded + turn(parts[p], p)
            rest = jnp.concatenate(parts[turned:], 1)
            rest = jnp.dot(rest, permutation, preferred_element_type=F32).astype(BF16)
            w_buf[ks, :] = folded + rest

    t_copy.wait()
    masked = []
    for i in range(rows):
        row = []
        for q in range(depth // LANES):
            group = t_buf[i, :, pl.ds(q * LANES, LANES)]
            kept = [
                jnp.where(labels[q] == own, group[g * BLOCK : (g + 1) * BLOCK], zero)
                for g, own in enumerate(own_labels[i])
            ]
            row.append(jnp.concatenate(kept, 0))
        masked.append(jnp.concatenate(row, 1))
    total[...] = jnp.dot(
        jnp.concatenate(masked, 0), w_buf[...], preferred_element_type=F32
    )

    lane_bits = bits_of(lane_block)
    occ_i_lane = jnp.zeros((8, LANES), I32)
    for i in range(rows):
        occ_i_lane = jnp.where(lane_block == i, occ_i[i], occ_i_lane)
    me = pair * REDS + red
    for g in range(occupied // 8):
        held = [turn(total[pl.ds(i * occupied + g * 8, 8), :], i) for i in range(rows)]
        skewed = pick(held, lane_bits)
        held = [turn(skewed[-d % 8], -d) for d in range(8)]
        held = pick(held, bits_of(occ_j[g] ^ occ_i_lane))
        for p in range(OWNERS):
            to = place((p * REDS + g * 8 // j_rows) ^ me)
            sums[to, pl.ds(g * 8 % j_rows, 8), :] = held[p]


def spread_kernel(offsets, j_in, i_in, *refs):
    arrays, (out, buf, sem) = refs[: len(offsets)], refs[-3:]
    pair = lax.axis_index("pair")
    j_side = j_in[...].astype(BF16)
    bits = bits_of(lax.broadcasted_iota(I32, j_side.shape, 1) // BLOCK)
    sources = [(ref, k, a) for ref, of in zip(arrays, offsets) for k, a in enumerate(of)]
    for n, (ref, k, a) in enumerate(sources):
        skewed = pick([turn(ref[k], d) for d in range(LABELS)], bits)
        for i in range(8):
            wanted = jnp.broadcast_to(i_in[pl.ds(8 * a + i, 1), :], j_side.shape).astype(BF16)
            buf[n, i] = jnp.where(wanted == j_side, skewed[-i % LABELS], jnp.zeros((), BF16))
        pltpu.make_async_copy(buf.at[n], out.at[pl.ds((pair ^ a) * 8, 8)], sem).start()
    pltpu.make_async_copy(buf, buf, sem).wait()


def spread(j_side, i_side, blocks, so_far=None):
    offsets, arrays = [of for of, _ in blocks], [array for _, array in blocks]
    count = sum(len(of) for of in offsets)
    occupied, j_rows = i_side.shape[0], j_side.shape[0]
    vmem, hbm = pl.BlockSpec(memory_space=pltpu.VMEM), pl.BlockSpec(memory_space=pltpu.HBM)
    earlier = [] if so_far is None else [so_far]
    return pl.pallas_call(
        functools.partial(spread_kernel, offsets),
        out_shape=jax.ShapeDtypeStruct((occupied, j_rows, LANES), BF16),
        in_specs=[vmem] * (2 + len(arrays)) + [hbm] * len(earlier),
        out_specs=hbm,
        scratch_shapes=[
            pltpu.VMEM((count, 8, j_rows, LANES), BF16),
            pltpu.SemaphoreType.DMA,
        ],
        input_output_aliases={2 + len(arrays): 0} if earlier else {},
        compiler_params=pltpu.CompilerParams(vmem_limit_bytes=8 * 2**20),
        cost_estimate=pl.CostEstimate(
            flops=10**6, bytes_accessed=2 * count * 8 * j_rows * LANES, transcendentals=0
        ),
        name="spread",
    )(j_side, i_side, *arrays, *earlier)


def in_hbm(*arrays):
    return [pltpu.with_memory_space_constraint(a, pltpu.HBM) for a in arrays]


def fast(amplitudes, integrals, occ_irrep, vir_irrep, cd_orbitals, ab_orbitals):
    rows, occupied, depth = amplitudes.shape
    j_rows = occupied // REDS
    vmem, hbm = pl.BlockSpec(memory_space=pltpu.VMEM), pl.BlockSpec(memory_space=pltpu.HBM)
    sums, j_side, i_side = pl.pallas_call(
        sums_kernel,
        out_shape=(
            jax.ShapeDtypeStruct((OWNERS * REDS, j_rows, LANES), F32),
            jax.ShapeDtypeStruct((j_rows, LANES), F32),
            jax.ShapeDtypeStruct((occupied, LANES), F32),
        ),
        in_specs=[hbm] * 5,
        out_specs=(vmem,) * 3,
        scratch_shapes=[
            pltpu.VMEM(amplitudes.shape, BF16),
            pltpu.VMEM(integrals.shape, BF16),
            pltpu.VMEM((depth, LANES), BF16),
            pltpu.VMEM((rows * occupied, LANES), F32),
            pltpu.SMEM(occ_irrep.shape, I32),
            pltpu.VMEM(vir_irrep.shape, I32),
            pltpu.VMEM(cd_orbitals.shape, I32),
            pltpu.SemaphoreType.DMA,
            pltpu.SemaphoreType.DMA((V_CHUNKS,)),
            pltpu.SemaphoreType.DMA((3,)),
        ],
        compiler_params=pltpu.CompilerParams(vmem_limit_bytes=32 * 2**20),
        name="sums",
    )(*in_hbm(occ_irrep, vir_irrep, cd_orbitals, amplitudes, integrals))

    def swap(block, pattern):
        pairs = [(d, d ^ pattern) for d in range(OWNERS * REDS)]
        return lax.ppermute(block, ("pair", "red"), pairs)

    shape = (2, 2, 2, 2, 2, j_rows, LANES)
    sums = sums.reshape(shape)
    chip = sums[0] + swap(sums[1], CORE)
    low = swap(chip[0, 1], LOW)
    across = swap(chip[1, 0], X)
    corner = swap(chip[1, 1], X ^ LOW)
    done = jnp.stack([(chip[0, 0] + across).astype(BF16), (low + corner).astype(BF16)])
    both = jnp.stack([done[:, :, 0], swap(done[:, :, 1], HIGH)]).reshape(4, 2, j_rows, LANES)
    side = swap(both[:, 1], Y)
    out = spread(j_side, i_side, [((0, 2, 4, 6), both[:, 0])])
    return spread(j_side, i_side, [((1, 3, 5, 7), side)], out)


def solution(mesh):
    def local(amplitudes, integrals, occ_irrep, vir_irrep, cd_orbitals, ab_orbitals):
        sizes = mesh.shape["pair"], mesh.shape["red"], amplitudes.shape[0], ab_orbitals.shape[1]
        form = fast if sizes == (OWNERS, REDS, 8, LANES) else general
        return form(amplitudes, integrals, occ_irrep, vir_irrep, cd_orbitals, ab_orbitals)

    in_specs = (P("pair", None, "red"), P("red", None), P(), P(), P(None, "red"), P(None, "pair"))
    out_specs = P(None, "red", "pair")
    return jax.shard_map(local, mesh=mesh, in_specs=in_specs, out_specs=out_specs, check_vma=False)
```

```python
import functools

import jax
import jax.numpy as jnp
from jax import lax
from jax.experimental import pallas as pl
from jax.experimental.pallas import tpu as pltpu
from jax.sharding import PartitionSpec as P

LABELS = 8
LANES = 128
BLOCK = LANES // LABELS
F32, BF16, I32 = jnp.float32, jnp.bfloat16, jnp.int32


def pair_labels(orbitals, vir_irrep):
    labels = lax.broadcasted_iota(I32, (1, vir_irrep.shape[0]), 1)
    first = jnp.sum(jnp.where(orbitals[0][:, None] == labels, vir_irrep[None, :], 0), axis=1)
    second = jnp.sum(jnp.where(orbitals[1][:, None] == labels, vir_irrep[None, :], 0), axis=1)
    return jnp.bitwise_xor(first, second)


def general(amplitudes, integrals, occ_irrep, vir_irrep, cd_orbitals, ab_orbitals):
    own_rows, occupied, depth = amplitudes.shape
    width = ab_orbitals.shape[1]
    owners = integrals.shape[1] // width
    block = width // LABELS
    own_irrep = lax.dynamic_slice_in_dim(occ_irrep, lax.axis_index("pair") * own_rows, own_rows, 0)
    pair_irrep = jnp.bitwise_xor(own_irrep[:, None], occ_irrep[None, :])
    cd_irrep = pair_labels(cd_orbitals, vir_irrep)
    masked = jnp.where(pair_irrep[:, :, None] == cd_irrep, amplitudes, jnp.zeros((), BF16))
    sums = jnp.dot(
        masked.reshape(own_rows * occupied, depth), integrals, preferred_element_type=F32
    ).reshape(own_rows, occupied, owners, LABELS, block)
    label = lax.broadcasted_iota(I32, (LABELS, 1), 0)
    kept = jnp.where(pair_irrep[:, :, None, None, None] == label, sums, 0.0).sum(axis=3)
    summed = lax.psum_scatter(kept, "red", scatter_dimension=1, tiled=True)
    moved = lax.all_to_all(
        summed.astype(BF16), "pair", split_axis=2, concat_axis=0, tiled=True
    )[:, :, 0, None, :]
    j_rows = moved.shape[1]
    j_irrep = lax.dynamic_slice_in_dim(occ_irrep, lax.axis_index("red") * j_rows, j_rows, 0)
    out_irrep = jnp.bitwise_xor(occ_irrep[:, None], j_irrep[None, :])
    out = jnp.where(out_irrep[:, :, None, None] == label, moved, jnp.zeros((), BF16))
    return out.reshape(occupied, j_rows, width)


OWNERS = 8
REDS = 4
V_CHUNKS = 2
BY_PRODUCT = 1


def place(offset):
    core, x, y, low, high = [(offset >> b) & 1 for b in range(5)]
    return ((((core ^ y ^ low ^ high) * 2 + x) * 2 + low) * 2 + y) * 2 + high


CORE, X, Y, LOW, HIGH = 0b00001, 0b00010, 0b00101, 0b01001, 0b10001


def pick(vectors, shift_bits):
    for b in range(3):
        vectors = [
            jnp.where(shift_bits[b], vectors[(d + 2**b) % 8], vectors[d]) for d in range(8)
        ]
    return vectors


def turn(vector, blocks):
    return pltpu.roll(vector, blocks % LABELS * BLOCK, 1) if blocks % LABELS else vector


def bits_of(labels):
    return [((labels >> b) & 1) == 1 for b in range(3)]


def sums_kernel(
    occ_hbm, vir_hbm, cd_hbm, t_hbm, v_hbm, sums, j_out, i_out,
    t_buf, v_buf, w_buf, total, occ, vir, cd, t_sem, v_sem, s_sem,
):
    rows, occupied, depth = t_buf.shape
    span = depth // V_CHUNKS
    small = [
        pltpu.make_async_copy(source, target, s_sem.at[n])
        for n, (source, target) in enumerate(((occ_hbm, occ), (vir_hbm, vir), (cd_hbm, cd)))
    ]
    v_copies = [
        pltpu.make_async_copy(
            v_hbm.at[pl.ds(c * span, span), :], v_buf.at[pl.ds(c * span, span), :], v_sem.at[c]
        )
        for c in range(V_CHUNKS)
    ]
    t_copy = pltpu.make_async_copy(t_hbm, t_buf, t_sem)
    for copy in (*small, *v_copies, t_copy):
        copy.start()
    pair, red = lax.axis_index("pair"), lax.axis_index("red")
    for copy in small:
        copy.wait()

    zero, one = jnp.zeros((), BF16), jnp.ones((), BF16)
    sublane = lax.broadcasted_iota(I32, (8, LANES), 0)
    lane_block = lax.broadcasted_iota(I32, (8, LANES), 1) // BLOCK

    def column(first):
        value = jnp.full((8, LANES), occ[first], I32)
        for s in range(1, 8):
            value = jnp.where(sublane == s, occ[first + s], value)
        return value

    occ_j = [column(8 * g) for g in range(occupied // 8)]
    occ_i = [occ[pair * rows + i] for i in range(rows)]

    j_rows = occupied // REDS
    for g in range(j_rows // 8):
        value = column(red * j_rows + 8 * g) ^ lane_block
        j_out[pl.ds(8 * g, 8), :] = value.astype(F32)
    for a in range(OWNERS):
        i_out[pl.ds(8 * a, 8), :] = column((pair ^ a) * rows).astype(F32)

    pieces = vir.shape[0] // LANES
    table = [
        jnp.broadcast_to(vir[pl.ds(LANES * n, LANES)].reshape(1, LANES), (8, LANES))
        for n in range(pieces)
    ]
    sub_block = lax.broadcasted_iota(I32, (BLOCK, LANES), 0) // BLOCK
    block_rows = [(sub_block + b).astype(F32).astype(BF16) for b in range(LABELS)]
    labels, masks = [], []
    for z in range(depth // LANES // 4):
        index = jnp.concatenate([cd[:, pl.ds((4 * z + u) * LANES, LANES)] for u in range(4)], 0)
        within, piece = index % LANES, index // LANES
        found = jnp.take_along_axis(table[0], within, axis=1)
        for n in range(1, pieces):
            found = jnp.where(piece == n, jnp.take_along_axis(table[n], within, axis=1), found)
        found = (found ^ pltpu.roll(found, 7, 0)).astype(F32)
        for u in range(4):
            label = jnp.broadcast_to(found[2 * u : 2 * u + 1], (BLOCK, LANES)).astype(BF16)
            labels.append(label)
            own = [jnp.where(label == row, one, zero) for row in block_rows]
            masks.append(jnp.concatenate(own, 0).T)
    own_labels = [
        [
            (jnp.concatenate(occ_j[g : g + 2], 0) ^ occ_i[i]).astype(F32).astype(BF16)
            for g in range(0, occupied // 8, 2)
        ]
        for i in range(rows)
    ]

    turned = OWNERS - BY_PRODUCT
    row = lax.broadcasted_iota(I32, (BY_PRODUCT * LANES, LANES), 0)
    lane = lax.broadcasted_iota(I32, (BY_PRODUCT * LANES, LANES), 1)
    target = (row + (row // LANES + turned) * BLOCK) % LANES
    permutation = jnp.where(target == lane, 1.0, 0.0).astype(BF16)
    for c in range(V_CHUNKS):
        v_copies[c].wait()
        for q in range(c * span // LANES, (c + 1) * span // LANES):
            ks = pl.ds(q * LANES, LANES)
            parts = [masks[q] * v_buf[ks, pl.ds(p * LANES, LANES)] for p in range(OWNERS)]
            folded = parts[0]
            for p in range(1, turned):
                folded = folded + turn(parts[p], p)
            rest = jnp.concatenate(parts[turned:], 1)
            rest = jnp.dot(rest, permutation, preferred_element_type=F32).astype(BF16)
            w_buf[ks, :] = folded + rest

    t_copy.wait()
    masked = []
    for i in range(rows):
        row = []
        for q in range(depth // LANES):
            group = t_buf[i, :, pl.ds(q * LANES, LANES)]
            kept = [
                jnp.where(labels[q] == own, group[g * BLOCK : (g + 1) * BLOCK], zero)
                for g, own in enumerate(own_labels[i])
            ]
            row.append(jnp.concatenate(kept, 0))
        masked.append(jnp.concatenate(row, 1))
    total[...] = jnp.dot(
        jnp.concatenate(masked, 0), w_buf[...], preferred_element_type=F32
    )

    lane_bits = bits_of(lane_block)
    occ_i_lane = jnp.zeros((8, LANES), I32)
    for i in range(rows):
        occ_i_lane = jnp.where(lane_block == i, occ_i[i], occ_i_lane)
    me = pair * REDS + red
    for g in range(occupied // 8):
        held = [turn(total[pl.ds(i * occupied + g * 8, 8), :], i) for i in range(rows)]
        skewed = pick(held, lane_bits)
        held = [turn(skewed[-d % 8], -d) for d in range(8)]
        held = pick(held, bits_of(occ_j[g] ^ occ_i_lane))
        for p in range(OWNERS):
            to = place((p * REDS + g * 8 // j_rows) ^ me)
            sums[to, pl.ds(g * 8 % j_rows, 8), :] = held[p]


def spread_kernel(offsets, j_in, i_in, *refs):
    arrays, (out, buf, sem) = refs[: len(offsets)], refs[-3:]
    pair = lax.axis_index("pair")
    j_side = j_in[...].astype(BF16)
    bits = bits_of(lax.broadcasted_iota(I32, j_side.shape, 1) // BLOCK)
    sources = [(ref, k, a) for ref, of in zip(arrays, offsets) for k, a in enumerate(of)]
    for n, (ref, k, a) in enumerate(sources):
        skewed = pick([turn(ref[k], d) for d in range(LABELS)], bits)
        for i in range(8):
            wanted = jnp.broadcast_to(i_in[pl.ds(8 * a + i, 1), :], j_side.shape).astype(BF16)
            buf[n, i] = jnp.where(wanted == j_side, skewed[-i % LABELS], jnp.zeros((), BF16))
        pltpu.make_async_copy(buf.at[n], out.at[pl.ds((pair ^ a) * 8, 8)], sem).start()
    pltpu.make_async_copy(buf, buf, sem).wait()


def spread(j_side, i_side, blocks, so_far=None):
    offsets, arrays = [of for of, _ in blocks], [array for _, array in blocks]
    count = sum(len(of) for of in offsets)
    occupied, j_rows = i_side.shape[0], j_side.shape[0]
    vmem, hbm = pl.BlockSpec(memory_space=pltpu.VMEM), pl.BlockSpec(memory_space=pltpu.HBM)
    earlier = [] if so_far is None else [so_far]
    return pl.pallas_call(
        functools.partial(spread_kernel, offsets),
        out_shape=jax.ShapeDtypeStruct((occupied, j_rows, LANES), BF16),
        in_specs=[vmem] * (2 + len(arrays)) + [hbm] * len(earlier),
        out_specs=hbm,
        scratch_shapes=[
            pltpu.VMEM((count, 8, j_rows, LANES), BF16),
            pltpu.SemaphoreType.DMA,
        ],
        input_output_aliases={2 + len(arrays): 0} if earlier else {},
        compiler_params=pltpu.CompilerParams(vmem_limit_bytes=8 * 2**20),
        cost_estimate=pl.CostEstimate(
            flops=10**6, bytes_accessed=2 * count * 8 * j_rows * LANES, transcendentals=0
        ),
        name="spread",
    )(j_side, i_side, *arrays, *earlier)


def in_hbm(*arrays):
    return [pltpu.with_memory_space_constraint(a, pltpu.HBM) for a in arrays]


def fast(amplitudes, integrals, occ_irrep, vir_irrep, cd_orbitals, ab_orbitals):
    rows, occupied, depth = amplitudes.shape
    j_rows = occupied // REDS
    vmem, hbm = pl.BlockSpec(memory_space=pltpu.VMEM), pl.BlockSpec(memory_space=pltpu.HBM)
    sums, j_side, i_side = pl.pallas_call(
        sums_kernel,
        out_shape=(
            jax.ShapeDtypeStruct((OWNERS * REDS, j_rows, LANES), F32),
            jax.ShapeDtypeStruct((j_rows, LANES), F32),
            jax.ShapeDtypeStruct((occupied, LANES), F32),
        ),
        in_specs=[hbm] * 5,
        out_specs=(vmem,) * 3,
        scratch_shapes=[
            pltpu.VMEM(amplitudes.shape, BF16),
            pltpu.VMEM(integrals.shape, BF16),
            pltpu.VMEM((depth, LANES), BF16),
            pltpu.VMEM((rows * occupied, LANES), F32),
            pltpu.SMEM(occ_irrep.shape, I32),
            pltpu.VMEM(vir_irrep.shape, I32),
            pltpu.VMEM(cd_orbitals.shape, I32),
            pltpu.SemaphoreType.DMA,
            pltpu.SemaphoreType.DMA((V_CHUNKS,)),
            pltpu.SemaphoreType.DMA((3,)),
        ],
        compiler_params=pltpu.CompilerParams(vmem_limit_bytes=32 * 2**20),
        name="sums",
    )(*in_hbm(occ_irrep, vir_irrep, cd_orbitals, amplitudes, integrals))

    def swap(block, pattern):
        pairs = [(d, d ^ pattern) for d in range(OWNERS * REDS)]
        return lax.ppermute(block, ("pair", "red"), pairs)

    shape = (2, 2, 2, 2, 2, j_rows, LANES)
    sums = sums.reshape(shape)
    chip = sums[0] + swap(sums[1], CORE)
    low = swap(chip[0, 1], LOW)
    across = swap(chip[1, 0], X)
    corner = swap(chip[1, 1], X ^ LOW)
    done = jnp.stack([(chip[0, 0] + across).astype(BF16), (low + corner).astype(BF16)])
    both = jnp.stack([done[:, :, 0], swap(done[:, :, 1], HIGH)]).reshape(4, 2, j_rows, LANES)
    side = swap(both[:, 1], Y)
    out = spread(j_side, i_side, [((0, 2, 4, 6), both[:, 0])])
    return spread(j_side, i_side, [((1, 3, 5, 7), side)], out)


def solution(mesh):
    def local(amplitudes, integrals, occ_irrep, vir_irrep, cd_orbitals, ab_orbitals):
        sizes = mesh.shape["pair"], mesh.shape["red"], amplitudes.shape[0], ab_orbitals.shape[1]
        form = fast if sizes == (OWNERS, REDS, 8, LANES) else general
        return form(amplitudes, integrals, occ_irrep, vir_irrep, cd_orbitals, ab_orbitals)

    in_specs = (P("pair", None, "red"), P("red", None), P(), P(), P(None, "red"), P(None, "pair"))
    out_specs = P(None, "red", "pair")
    return jax.shard_map(local, mesh=mesh, in_specs=in_specs, out_specs=out_specs, check_vma=False)
```
